128 devices in a mesh: row: 8 (over z, y_lo), col: 16 (over y_hi, x, core).
Axes of the slice: x: 4, y: 4 (y_hi: 2, y_lo: 2; y = y_hi * 2 + y_lo), z: 4, core: 2. Of those that a mesh axis runs over, the one named last changes fastest.
Arguments:
- features: bfloat16 [64, 128, 1024], P('row', 'col'), may hold values from -6 to 6
- gate_branch: bfloat16 [64, 128, 1024], P('row', 'col'), may hold values from -6 to 6
- w_row_proj: bfloat16 [1024, 128], replicated, may hold values from -0.1875 to 0.1875
- w_dt_row: bfloat16 [2, 32, 1024], P(None, None, 'col'), may hold values from -1 to 1
- dt_bias_row: float32 [2, 1024], P(None, 'col'), may hold values from -5 to -1
- rate_row: float32 [2, 1024, 16], P(None, 'col'), may hold values from 0.01 to 1
- skip_row: float32 [1024], P('col'), may hold values from 0.5 to 1.5
- conv_kernel: float32 [3, 3, 1024], P(None, None, 'col'), may hold values from -2 to 2
- conv_bias: float32 [1024], P('col'), may hold values from -3 to 3
- w_col_proj: bfloat16 [1024, 128], replicated, may hold values from -0.1875 to 0.1875
- w_dt_col: bfloat16 [2, 32, 1024], P(None, None, 'row'), may hold values from -1 to 1
- dt_bias_col: float32 [2, 1024], P(None, 'row'), may hold values from -5 to -1
- rate_col: float32 [2, 1024, 16], P(None, 'row'), may hold values from 0.01 to 1
Outputs:
- block_out: bfloat16 [64, 128, 1024], P(None, 'col', 'row')
The draws below stay inside these ranges and needn't reach their ends.
All inputs are finite; a program needn't handle non-finite values.
Results may differ from the reference program's by a relative error of at most 0.0085.
The reference program's roundings to bfloat16 on the way (of `row_proj`, `gated_rows`, `mixed_cells` and `col_proj`) count: a program that leaves them out, or rounds other values in their place, can miss the bound.
Values may be sent and summed in bfloat16 or wider, within the bound.
A program may use at most 64 MiB of HBM per device.

```python
import math
import jax
import jax.numpy as jnp
from jax import lax

E = 1024
STATE = 16
RANK = 32
PROJ = 128
H = 64
W = 128


def block_scale(stream_key, shape, split, low, largest):
    factor_of, own = 1.0, jax.random.fold_in(stream_key, 6)
    for axis_at, blocks in split:
        heights = jnp.exp(jax.random.uniform(jax.random.fold_in(own, axis_at), (blocks,), jnp.float32, low / len(split), largest / len(split)))
        factor_of = factor_of * jnp.repeat(heights, shape[axis_at] // blocks).reshape([-1 if axis == axis_at else 1 for axis in range(len(shape))])
    return factor_of


def noise(rng, extent, deviation, most, pieces=(), held_as=jnp.bfloat16):
    entries = jax.random.normal(rng, extent, jnp.float32) * deviation
    if len(pieces) > 0:
        entries = block_scale(rng, extent, pieces, -0.22, 0.18) * entries
    return jnp.clip(entries, min=-most, max=most).astype(held_as)


def setup_inputs(seed: int = 0) -> dict:
    arg_keys = jax.random.split(jax.random.key(seed), 14)
    return {
        "features": noise(arg_keys[0], (H, W, E), 1.0, 6.0, ((0, 8), (1, 16))),
        "gate_branch": noise(arg_keys[1], (H, W, E), 1.0, 6.0, ((0, 8), (1, 16))),
        "w_row_proj": noise(arg_keys[2], (E, PROJ), E ** -0.5, 0.1875),
        "w_dt_row": noise(arg_keys[3], (2, RANK, E), RANK ** -0.5, 1.0, ((2, 16),)),
        "dt_bias_row": jnp.clip(-5.0 + 4.0 * jax.random.uniform(arg_keys[4], (2, E), jnp.float32) ** block_scale(arg_keys[4], (2, E), ((1, 16),), -0.2, 0.2), -5.0, -1.0),
        "rate_row": jnp.clip(jnp.exp(math.log(1.0) - 4.6051702 * jax.random.uniform(arg_keys[5], (2, E, STATE), jnp.float32) ** block_scale(arg_keys[5], (2, E, STATE), ((1, 16),), -0.2, 0.2)), 0.01, 1.0),
        "skip_row": jnp.clip(0.5 + 1.0 * jax.random.uniform(arg_keys[6], (E,), jnp.float32) ** block_scale(arg_keys[6], (E,), ((0, 16),), -0.2, 0.2), 0.5, 1.5),
        "conv_kernel": noise(arg_keys[7], (3, 3, E), 9 ** -0.5, 2.0, ((2, 16),), jnp.float32),
        "conv_bias": noise(arg_keys[8], (E,), 0.5, 3.0, ((0, 16),), jnp.float32),
        "w_col_proj": noise(arg_keys[9], (E, PROJ), E ** -0.5, 0.1875),
        "w_dt_col": noise(arg_keys[10], (2, RANK, E), RANK ** -0.5, 1.0, ((2, 8),)),
        "dt_bias_col": jnp.clip(-5.0 + 4.0 * jax.random.uniform(arg_keys[11], (2, E), jnp.float32) ** block_scale(arg_keys[11], (2, E), ((1, 8),), -0.2, 0.2), -5.0, -1.0),
        "rate_col": jnp.clip(jnp.exp(math.log(1.0) - 4.6051702 * jax.random.uniform(arg_keys[12], (2, E, STATE), jnp.float32) ** block_scale(arg_keys[12], (2, E, STATE), ((1, 8),), -0.2, 0.2)), 0.01, 1.0),
    }


def line_scan(inputs, step_sizes, drive_in, read_out, decay_rates, reverse):
    if reverse:
        inputs = jnp.flip(inputs, 1)
        step_sizes = jnp.flip(step_sizes, 1)
        drive_in = jnp.flip(drive_in, 1)
        read_out = jnp.flip(read_out, 1)
    line_count = inputs.shape[0]
    channels = inputs.shape[2]
    state_width = drive_in.shape[2]

    def advance(carried, slices):
        current, step_now, b_now, c_now = slices
        carried = jnp.exp(-step_now[:, :, None] * decay_rates[None]) * carried + (step_now * current)[:, :, None] * b_now[:, None, :]
        return carried, jnp.sum(carried * c_now[:, None, :], axis=2)

    initial = jnp.zeros((line_count, channels, state_width), jnp.float32)
    sequence = (jnp.swapaxes(inputs, 0, 1), jnp.swapaxes(step_sizes, 0, 1), jnp.swapaxes(drive_in, 0, 1), jnp.swapaxes(read_out, 0, 1))
    last_state, outputs = lax.scan(advance, initial, sequence)
    outputs = jnp.swapaxes(outputs, 0, 1)
    if reverse:
        outputs = jnp.flip(outputs, 1)
    return outputs


def both_ways(values, projections, step_weight, step_bias, decay_rates, skip_gain):
    low_rank = step_weight.shape[1]
    state_width = decay_rates.shape[2]
    segment = low_rank + 2 * state_width
    line_count = values.shape[0]
    positions = values.shape[1]
    if skip_gain is None:
        summed = jnp.zeros(values.shape, jnp.float32)
    else:
        summed = skip_gain * values
    for direction in range(2):
        offset = direction * segment
        low_part = projections[:, :, offset:offset + low_rank]
        raw_steps = jnp.dot(low_part.reshape(-1, low_rank), step_weight[direction], preferred_element_type=jnp.float32)
        raw_steps = raw_steps.reshape(line_count, positions, -1)
        step_sizes = jax.nn.softplus(raw_steps + step_bias[direction])
        drive_in = projections[:, :, offset + low_rank:offset + low_rank + state_width].astype(jnp.float32)
        read_out = projections[:, :, offset + low_rank + state_width:offset + segment].astype(jnp.float32)
        summed = summed + line_scan(values, step_sizes, drive_in, read_out, decay_rates[direction], direction == 1)
    return summed


def reference(features, gate_branch, w_row_proj, w_dt_row, dt_bias_row, rate_row, skip_row, conv_kernel, conv_bias, w_col_proj, w_dt_col, dt_bias_col, rate_col):
    height, width_all, channels_all = features.shape
    row_proj = jnp.dot(features.reshape(-1, channels_all), w_row_proj, preferred_element_type=jnp.float32)
    row_proj = row_proj.astype(jnp.bfloat16).reshape(height, width_all, -1)
    row_mix = both_ways(features.astype(jnp.float32), row_proj, w_dt_row, dt_bias_row, rate_row, skip_row)
    gated_rows = (row_mix * jax.nn.silu(gate_branch.astype(jnp.float32))).astype(jnp.bfloat16)
    padded = jnp.pad(gated_rows.astype(jnp.float32), ((1, 1), (1, 1), (0, 0)))
    accumulated = jnp.zeros((height, width_all, channels_all), jnp.float32) + conv_bias
    for vertical in range(3):
        for lateral in range(3):
            accumulated = accumulated + conv_kernel[vertical, lateral] * padded[vertical:vertical + height, lateral:lateral + width_all]
    mixed_cells = jax.nn.silu(accumulated).astype(jnp.bfloat16)
    col_proj = jnp.dot(mixed_cells.reshape(-1, channels_all), w_col_proj, preferred_element_type=jnp.float32)
    col_proj = col_proj.astype(jnp.bfloat16).reshape(height, width_all, -1)
    column_out = both_ways(jnp.swapaxes(mixed_cells.astype(jnp.float32), 0, 1), jnp.swapaxes(col_proj, 0, 1), w_dt_col, dt_bias_col, rate_col, None)
    return jnp.swapaxes(column_out, 0, 1).astype(jnp.bfloat16)
```

```python
import functools

import jax
import jax.numpy as jnp
from jax import lax
from jax.experimental import pallas as pl
from jax.experimental.pallas import tpu as pltpu
from jax.sharding import PartitionSpec as P

F32, BF16 = jnp.float32, jnp.bfloat16
MESH = pl.DeviceIdType.MESH
N = 16
LOG2E = 1.4426950408889634


def softplus(v):
    return jnp.maximum(v, 0.0) + jnp.log1p(jnp.exp(-jnp.abs(v)))


def silu(v):
    return v / (1.0 + jnp.exp(-v))


def turn(v):
    groups = v.shape[0] // 8
    return jnp.concatenate([v[8 * g : 8 * g + 8] for g in reversed(range(groups))], axis=0)


def swap(v):
    return pltpu.roll(v, 64, 1)


def dot(a, b):
    return jnp.dot(a, b, preferred_element_type=F32)


def scan_block(states, rows, step_ref, x_ref, bc_ref, bc_row, rates, emit):
    states = list(states)
    for row, brow in zip(rows, bc_row):
        step = step_ref[pl.ds(row, 8), :]
        drive = step * x_ref[pl.ds(row, 8), :]
        out = None
        for n in range(N):
            decay = jnp.exp2(step * rates[n])
            states[n] = decay * states[n] + drive * bc_ref[pl.ds(brow, 8), n * 128 : (n + 1) * 128]
            term = states[n] * bc_ref[pl.ds(brow, 8), (N + n) * 128 : (N + n + 1) * 128]
            out = term if out is None else out + term
        emit(row, out)
    return tuple(states)


def kernel(
    R, C,
    f_ref, g_ref, wrp_ref, wcp_ref, wd_ref, par_ref,
    out_ref,
    sx, rx, rp, sh, rh, s3, r3, s4, r4, rp4,
    sel, bc, step, x2, y2, sg, z, acc, hz,
    px_s, px_r, pp_s, pp_r, h_s, h_r, m_s, m_r, c_s, c_r, q_s, q_r,
):
    r, c = lax.axis_index("row"), lax.axis_index("col")
    half = C // 2
    TW = half * 8
    lane = lax.broadcasted_iota(jnp.int32, (1, 128), 1)
    low = lane < 64

    def col_copy(src, dst, ss, rs, slot_src, slot_dst, to):
        return pltpu.make_async_remote_copy(
            src_ref=src.at[slot_src], dst_ref=dst.at[slot_dst], send_sem=ss, recv_sem=rs,
            device_id={"col": to}, device_id_type=MESH)

    def row_copy(src, dst, ss, rs, slot_src, slot_dst, to):
        return pltpu.make_async_remote_copy(
            src_ref=src.at[slot_src], dst_ref=dst.at[slot_dst], send_sem=ss, recv_sem=rs,
            device_id={"row": to}, device_id_type=MESH)

    barrier = pltpu.get_barrier_semaphore()

    @pl.loop(1, C)
    def _(k):
        pl.semaphore_signal(barrier, inc=1, device_id={"col": lax.rem(c + k, C)}, device_id_type=MESH)

    @pl.loop(1, R)
    def _(k):
        pl.semaphore_signal(barrier, inc=1, device_id={"row": lax.rem(r + k, R)}, device_id_type=MESH)

    ta = lax.broadcasted_iota(jnp.int32, (64, 64), 0)
    tb = lax.broadcasted_iota(jnp.int32, (64, 64), 1)
    perm = jnp.where(tb == lax.rem(ta, 8) * 8 + lax.div(ta, 8), 1.0, 0.0).astype(BF16)

    proj = dot(f_ref[...], wrp_ref[...]).astype(BF16)
    rp[c] = dot(perm, proj).astype(BF16)

    pl.semaphore_wait(barrier, C - 1 + R - 1)

    @pl.loop(1, C)
    def _(k):
        to = lax.rem(c + k, C)
        col_copy(rp, rp, pp_s.at[to], pp_r.at[c], c, c, to).start()

    for j in range(half):
        fj = dot(perm, f_ref[:, 128 * j : 128 * j + 128])
        gj = dot(perm, g_ref[:, 128 * j : 128 * j + 128])
        sx[2 * j] = jnp.where(low, fj, swap(gj)).astype(BF16)
        sx[2 * j + 1] = jnp.where(low, swap(fj), gj).astype(BF16)

    @pl.loop(1, C)
    def _(k):
        to = lax.rem(c + k, C)
        col_copy(sx, rx, px_s.at[to], px_r.at[c], to, c, to).start()

    rx[c] = sx[c]

    kk = lax.broadcasted_iota(jnp.int32, (128, 128), 0)
    ll = lax.broadcasted_iota(jnp.int32, (128, 128), 1)
    kl = kk - jnp.where(ll >= 64, 64, 0)
    for n in range(2 * N):
        at = slice(n * 128, n * 128 + 128)
        sel[0, :, at] = jnp.where(kl == 32 + n, 1.0, 0.0).astype(BF16)
        sel[1, :, at] = jnp.where(kk == 32 + n, 1.0, 0.0).astype(BF16)
        sel[2, :, at] = jnp.where(kk == 96 + n, 1.0, 0.0).astype(BF16)

    base = jnp.where(c < half, c, C - 1 - c)

    @pl.loop(0, half)
    def _(k):
        b = lax.rem(base + k, half)
        o = C - 1 - b
        for s in (b, o):
            @pl.when(s != c)
            def _():
                col_copy(rp, rp, pp_s.at[s], pp_r.at[s], s, s, s).wait_recv()
        pb, po = rp[b].astype(F32), rp[o].astype(F32)
        for at, mine, other in ((b, pb, po), (o, po, pb)):
            src = jnp.where(low, mine, turn(other)).astype(BF16)
            rows = pl.ds(pl.multiple_of(at * 64, 64), 64)
            step[rows, :] = softplus(dot(src, wd_ref[:, 0:128]) + par_ref[0:1, :])
            for q in range(8):
                bc[rows, q * 512 : q * 512 + 512] = dot(src, sel[0, :, q * 512 : q * 512 + 512])

    @pl.loop(0, half)
    def _(k):
        b = lax.rem(base + k, half)
        o = C - 1 - b
        for s in (b, o):
            @pl.when(s != c)
            def _():
                col_copy(sx, rx, px_s.at[s], px_r.at[s], s, s, s).wait_recv()
        vb, vo = rx[b].astype(F32), rx[o].astype(F32)
        tb_, to_ = turn(vb), turn(vo)
        brow, orow = pl.ds(pl.multiple_of(b * 64, 64), 64), pl.ds(pl.multiple_of(o * 64, 64), 64)
        x2[brow, :] = jnp.where(low, vb, swap(to_))
        x2[orow, :] = jnp.where(low, vo, swap(tb_))
        sg[brow, :] = silu(jnp.where(low, swap(vb), to_))

    rates = [par_ref[16 + n : 17 + n, :] for n in range(N)]
    zero_states = tuple(jnp.zeros((8, 128), F32) for _ in range(N))

    def put(row, out):
        y2[pl.ds(row, 8), :] = out

    def row_body(i, states):
        rows = [pl.multiple_of(i * 64 + 8 * u, 8) for u in range(8)]
        return scan_block(states, rows, step, x2, bc, rows, rates, put)

    lax.fori_loop(0, C, row_body, zero_states)

    skip = par_ref[1:2, :]
    z[0:8, :] = jnp.zeros((8, 128), F32)
    for b in range(half):
        here, there = slice(64 * b, 64 * b + 64), slice(64 * (C - 1 - b), 64 * (C - b))
        mix = skip * x2[here, :] + y2[here, :] + swap(turn(y2[there, :]))
        gated = (mix * sg[here, :]).astype(BF16).astype(F32)
        z[64 * b + 8 : 64 * b + 72, :] = gated
    z[8 * TW + 8 : 8 * TW + 16, :] = swap(z[8 * TW : 8 * TW + 8, :])

    sh[0] = z[pl.ds(8 + 7, TW, stride=8), :].astype(BF16)
    sh[1] = z[pl.ds(8, TW, stride=8), :].astype(BF16)
    down = row_copy(sh, rh, h_s.at[0], h_r.at[0], 0, 0, lax.rem(r + 1, R))
    up = row_copy(sh, rh, h_s.at[1], h_r.at[1], 1, 1, lax.rem(r + R - 1, R))

    @pl.when(r < R - 1)
    def _():
        down.start()

    @pl.when(r > 0)
    def _():
        up.start()

    taps = [[par_ref[3 + 3 * i + j : 4 + 3 * i + j, :] for j in range(3)] for i in range(3)]
    sub = lax.broadcasted_iota(jnp.int32, (8, 128), 0)
    conv_bias = par_ref[2:3, :]

    @pl.loop(0, half)
    def _(b):
        group = [z[pl.ds(pl.multiple_of(b * 64 + 8 * u, 8), 8), :] for u in range(10)]
        for u in range(8):
            q = [taps[i][0] * group[u] + taps[i][1] * group[u + 1] + taps[i][2] * group[u + 2]
                 for i in range(3)]
            above = jnp.where(sub == 0, 0.0, pltpu.roll(q[0], 1, 0))
            below = jnp.where(sub == 7, 0.0, pltpu.roll(q[2], 7, 0))
            acc[pl.ds(pl.multiple_of(b * 64 + 8 * u, 8), 8), :] = conv_bias + above + q[1] + below

    @pl.when(r == 0)
    def _():
        rh[0] = jnp.zeros((TW, 128), BF16)

    @pl.when(r == R - 1)
    def _():
        rh[1] = jnp.zeros((TW, 128), BF16)

    @pl.when(r > 0)
    def _():
        down.wait_recv()

    @pl.when(r < R - 1)
    def _():
        up.wait_recv()

    for side, i, first in ((0, 0, 0), (1, 2, 7)):
        hz[0:8, :] = jnp.zeros((8, 128), F32)
        halo = rh[side].astype(F32)
        hz[8 : 8 + TW, :] = halo
        hz[8 + TW : 16 + TW, :] = swap(jnp.broadcast_to(halo[TW - 1 : TW, :], (8, 128)))
        add = (taps[i][0] * hz[7 : 7 + TW, :] + taps[i][1] * halo + taps[i][2] * hz[9 : 9 + TW, :])
        at = pl.ds(first, TW, stride=8)
        acc[at, :] = acc[at, :] + add

    for b in range(half):
        cells = silu(acc[64 * b : 64 * b + 64, :]).astype(BF16).astype(F32)
        near, far = cells[0:32, :], swap(turn(cells[32:64, :]))
        s3[b] = jnp.where(low, near, far).astype(BF16)
        s3[C - 1 - b] = jnp.where(low, far, near).astype(BF16)

    @pl.loop(1, C)
    def _(k):
        to = lax.rem(c + k, C)
        col_copy(s3, r3, m_s.at[to], m_r.at[c], to, c, to).start()

    r3[c] = s3[c]

    @pl.loop(0, C)
    def _(s):
        @pl.when(s != c)
        def _():
            col_copy(s3, r3, m_s.at[s], m_r.at[s], s, s, s).wait_recv()

    total = jnp.zeros((64, 128), F32)
    for j in range(R):
        one, two = r3[2 * j].astype(F32), r3[2 * j + 1].astype(F32)
        first = jnp.where(low, one, swap(two))
        second = jnp.where(low, swap(one), two)
        tokens = jnp.concatenate([first, turn(second)], axis=0).astype(BF16)
        tokens = dot(perm, tokens).astype(BF16)
        s4[j] = tokens
        total = total + dot(tokens, wcp_ref[128 * j : 128 * j + 128, :])
    rp4[r] = total.astype(BF16)

    @pl.loop(1, R)
    def _(k):
        to = lax.rem(r + k, R)
        row_copy(rp4, rp4, q_s.at[to], q_r.at[r], r, r, to).start()

    @pl.loop(1, R)
    def _(k):
        to = lax.rem(r + k, R)
        row_copy(s4, r4, c_s.at[to], c_r.at[r], to, r, to).start()

    r4[r] = s4[r]

    HT = 64 * R

    @pl.loop(0, R)
    def _(k):
        s = lax.rem(r + k, R)

        @pl.when(s != r)
        def _():
            row_copy(rp4, rp4, q_s.at[s], q_r.at[s], s, s, s).wait_recv()

        src = rp4[s]
        for d in range(2):
            rows = pl.ds(pl.multiple_of(d * HT + s * 64, 64), 64)
            raw = dot(src, wd_ref[:, 128 + 128 * d : 256 + 128 * d])
            step[rows, :] = softplus(raw + par_ref[12 + d : 13 + d, :])
            for q in range(8):
                bc[rows, q * 512 : q * 512 + 512] = dot(src, sel[1 + d, :, q * 512 : q * 512 + 512])

    @pl.loop(0, R)
    def _(k):
        s = lax.rem(r + k, R)

        @pl.when(s != r)
        def _():
            row_copy(s4, r4, c_s.at[s], c_r.at[s], s, s, s).wait_recv()

        cells = r4[s].astype(F32)
        for d in range(2):
            x2[pl.ds(pl.multiple_of(d * HT + s * 64, 64), 64), :] = cells

    for d in range(2):
        rates_d = [par_ref[32 + N * d + n : 33 + N * d + n, :] for n in range(N)]

        def col_body(i, states):
            block = i if d == 0 else R - 1 - i
            order = range(8) if d == 0 else range(7, -1, -1)
            rows = [pl.multiple_of(d * HT + block * 64 + 8 * u, 8) for u in order]
            return scan_block(states, rows, step, x2, bc, rows, rates_d, put)

        lax.fori_loop(0, R, col_body, zero_states)

    for b in range(R):
        out_ref[64 * b : 64 * b + 64, :] = (
            y2[64 * b : 64 * b + 64, :] + y2[HT + 64 * b : HT + 64 * b + 64, :]).astype(BF16)

    @pl.loop(1, C)
    def _(k):
        to = lax.rem(c + k, C)
        col_copy(rp, rp, pp_s.at[to], pp_r.at[c], c, c, to).wait_send()
        col_copy(sx, rx, px_s.at[to], px_r.at[c], to, c, to).wait_send()
        col_copy(s3, r3, m_s.at[to], m_r.at[c], to, c, to).wait_send()

    @pl.loop(1, R)
    def _(k):
        to = lax.rem(r + k, R)
        row_copy(rp4, rp4, q_s.at[to], q_r.at[r], r, r, to).wait_send()
        row_copy(s4, r4, c_s.at[to], c_r.at[r], to, r, to).wait_send()

    @pl.when(r < R - 1)
    def _():
        down.wait_send()

    @pl.when(r > 0)
    def _():
        up.wait_send()


def local(R, C, features, gate_branch, w_row_proj, w_dt_row, dt_bias_row, rate_row, skip_row,
          conv_kernel, conv_bias, w_col_proj, w_dt_col, dt_bias_col, rate_col):
    E = features.shape[2]
    both = lambda v: jnp.concatenate([v, v], axis=-1)
    flipped = conv_kernel[:, ::-1, :]
    params = jnp.concatenate(
        [
            dt_bias_row.reshape(1, 128),
            both(skip_row)[None],
            both(conv_bias)[None],
            jnp.concatenate([conv_kernel, flipped], axis=-1).reshape(9, 128),
            dt_bias_col,
            jnp.zeros((2, 128), F32),
            jnp.transpose(rate_row, (2, 0, 1)).reshape(N, 128) * -LOG2E,
            jnp.transpose(rate_col, (0, 2, 1)).reshape(2 * N, 128) * -LOG2E,
        ],
        axis=0,
    )
    zr = jnp.zeros((32, 64), BF16)
    wide = jnp.concatenate(
        [
            jnp.concatenate([w_dt_row[0], zr, w_dt_col[0], jnp.zeros((32, 128), BF16)], axis=1),
            jnp.zeros((32, 384), BF16),
            jnp.concatenate([zr, w_dt_row[1], jnp.zeros((32, 128), BF16), w_dt_col[1]], axis=1),
            jnp.zeros((32, 384), BF16),
        ],
        axis=0,
    )
    dma = pltpu.SemaphoreType.DMA
    TW = 4 * C
    out = pl.pallas_call(
        functools.partial(kernel, R, C),
        out_shape=jax.ShapeDtypeStruct((64 * R, 128), BF16),
        in_specs=[pl.BlockSpec(memory_space=pltpu.VMEM)] * 6,
        out_specs=pl.BlockSpec(memory_space=pltpu.VMEM),
        scratch_shapes=[
            pltpu.VMEM((C, 64, 128), BF16),
            pltpu.VMEM((C, 64, 128), BF16),
            pltpu.VMEM((C, 64, 128), BF16),
            pltpu.VMEM((2, TW, 128), BF16),
            pltpu.VMEM((2, TW, 128), BF16),
            pltpu.VMEM((C, 32, 128), BF16),
            pltpu.VMEM((C, 32, 128), BF16),
            pltpu.VMEM((R, 64, 128), BF16),
            pltpu.VMEM((R, 64, 128), BF16),
            pltpu.VMEM((R, 64, 128), BF16),
            pltpu.VMEM((3, 128, 4096), BF16),
            pltpu.VMEM((64 * C, 4096), F32),
            pltpu.VMEM((64 * C, 128), F32),
            pltpu.VMEM((64 * C, 128), F32),
            pltpu.VMEM((64 * C, 128), F32),
            pltpu.VMEM((32 * C, 128), F32),
            pltpu.VMEM((32 * C + 16, 128), F32),
            pltpu.VMEM((32 * C, 128), F32),
            pltpu.VMEM((TW + 16, 128), F32),
            dma((C,)), dma((C,)), dma((C,)), dma((C,)), dma((2,)), dma((2,)),
            dma((C,)), dma((C,)), dma((R,)), dma((R,)), dma((R,)), dma((R,)),
        ],
        compiler_params=pltpu.CompilerParams(
            collective_id=0, has_side_effects=True, vmem_limit_bytes=48 << 20),
    )(features.reshape(64, E), gate_branch.reshape(64, E), w_row_proj, w_col_proj, wide, params)
    return out.reshape(8 * R, 8, 128)


def solution(mesh):
    return jax.shard_map(
        functools.partial(local, mesh.shape["row"], mesh.shape["col"]),
        mesh=mesh,
        in_specs=(
            P("row", "col", None),
            P("row", "col", None),
            P(),
            P(None, None, "col"),
            P(None, "col"),
            P(None, "col", None),
            P("col"),
            P(None, None, "col"),
            P("col"),
            P(),
            P(None, None, "row"),
            P(None, "row"),
            P(None, "row", None),
        ),
        out_specs=P(None, "col", "row"),
        check_vma=False,
    )
```

```python
import functools

import jax
import jax.numpy as jnp
from jax import lax
from jax.experimental import pallas as pl
from jax.experimental.pallas import tpu as pltpu
from jax.sharding import PartitionSpec as P

F32, BF16 = jnp.float32, jnp.bfloat16
MESH = pl.DeviceIdType.MESH
N = 16
LOG2E = 1.4426950408889634


def softplus(v):
    return jnp.maximum(v, 0.0) + jnp.log1p(jnp.exp(-jnp.abs(v)))


def silu(v):
    return v / (1.0 + jnp.exp(-v))


def turn(v):
    groups = v.shape[0] // 8
    return jnp.concatenate([v[8 * g : 8 * g + 8] for g in reversed(range(groups))], axis=0)


def swap(v):
    return pltpu.roll(v, 64, 1)


def dot(a, b):
    return jnp.dot(a, b, preferred_element_type=F32)


def scan_block(states, rows, step_ref, x_ref, bc_ref, bc_row, rates, emit):
    states = list(states)
    for row, brow in zip(rows, bc_row):
        step = step_ref[pl.ds(row, 8), :]
        drive = step * x_ref[pl.ds(row, 8), :]
        out = None
        for n in range(N):
            decay = jnp.exp2(step * rates[n])
            states[n] = decay * states[n] + drive * bc_ref[pl.ds(brow, 8), n * 128 : (n + 1) * 128]
            term = states[n] * bc_ref[pl.ds(brow, 8), (N + n) * 128 : (N + n + 1) * 128]
            out = term if out is None else out + term
        emit(row, out)
    return tuple(states)


def kernel(
    R, C,
    f_hbm, g_hbm, wrp_hbm, wdtr_hbm, biasr_hbm, rater_hbm, skip_hbm, kern_hbm, biask_hbm, wcp_hbm,
    wdtc_hbm, biasc_hbm, ratec_hbm,
    out_ref,
    f_ref, g_ref, wrp_ref, wdtr, biasr, rater, skipr, kern, biask, wcp_ref, wdtc, biasc, ratec,
    wd_ref, load_sem,
    sx, rx, rp, sh, rh, s3, r3, s4, r4, rp4,
    sel, bc, step, x2, y2, sg, z, acc, hz,
    px_s, px_r, pp_s, pp_r, h_s, h_r, m_s, m_r, c_s, c_r, q_s, q_r,
):
    r, c = lax.axis_index("row"), lax.axis_index("col")
    half = C // 2
    TW = half * 8
    lane = lax.broadcasted_iota(jnp.int32, (1, 128), 1)
    low = lane < 64

    def col_copy(src, dst, ss, rs, slot_src, slot_dst, to):
        return pltpu.make_async_remote_copy(
            src_ref=src.at[slot_src], dst_ref=dst.at[slot_dst], send_sem=ss, recv_sem=rs,
            device_id={"col": to}, device_id_type=MESH)

    def row_copy(src, dst, ss, rs, slot_src, slot_dst, to):
        return pltpu.make_async_remote_copy(
            src_ref=src.at[slot_src], dst_ref=dst.at[slot_dst], send_sem=ss, recv_sem=rs,
            device_id={"row": to}, device_id_type=MESH)

    sources = (f_hbm, wrp_hbm, g_hbm, wdtr_hbm, biasr_hbm, rater_hbm, skip_hbm, kern_hbm, biask_hbm,
               wcp_hbm, wdtc_hbm, biasc_hbm, ratec_hbm)
    targets = (f_ref, wrp_ref, g_ref, wdtr, biasr, rater, skipr, kern, biask,
               wcp_ref, wdtc, biasc, ratec)
    loads = [pltpu.make_async_copy(a, b, load_sem.at[i])
             for i, (a, b) in enumerate(zip(sources, targets))]
    for load in loads:
        load.start()

    sent = []

    def finish():
        for wait in sent:
            wait()

    def to_col(src, dst, ss, rs, own):
        def copy(k):
            to = lax.rem(c + k, C)
            return col_copy(src, dst, ss.at[to], rs.at[c], c if own else to, c, to)

        @pl.loop(1, C)
        def _(k):
            copy(k).start()

        @sent.append
        def _():
            @pl.loop(1, C)
            def _(k):
                copy(k).wait_send()

    def to_row(src, dst, ss, rs, own):
        def copy(k):
            to = lax.rem(r + k, R)
            return row_copy(src, dst, ss.at[to], rs.at[r], r if own else to, r, to)

        @pl.loop(1, R)
        def _(k):
            copy(k).start()

        @sent.append
        def _():
            @pl.loop(1, R)
            def _(k):
                copy(k).wait_send()

    barrier = pltpu.get_barrier_semaphore()

    @pl.loop(1, C)
    def _(k):
        pl.semaphore_signal(barrier, inc=1, device_id={"col": lax.rem(c + k, C)}, device_id_type=MESH)

    @pl.loop(1, R)
    def _(k):
        pl.semaphore_signal(barrier, inc=1, device_id={"row": lax.rem(r + k, R)}, device_id_type=MESH)

    ta = lax.broadcasted_iota(jnp.int32, (64, 64), 0)
    tb = lax.broadcasted_iota(jnp.int32, (64, 64), 1)
    perm = jnp.where(tb == lax.rem(ta, 8) * 8 + lax.div(ta, 8), 1.0, 0.0).astype(BF16)

    loads[0].wait()
    loads[1].wait()
    proj = dot(f_ref[...], wrp_ref[...]).astype(BF16)
    rp[c] = dot(perm, proj).astype(BF16)

    pl.semaphore_wait(barrier, C - 1 + R - 1)

    to_col(rp, rp, pp_s, pp_r, True)

    loads[2].wait()
    for j in range(half):
        fj = dot(perm, f_ref[:, 128 * j : 128 * j + 128])
        gj = dot(perm, g_ref[:, 128 * j : 128 * j + 128])
        sx[2 * j] = jnp.where(low, fj, swap(gj)).astype(BF16)
        sx[2 * j + 1] = jnp.where(low, swap(fj), gj).astype(BF16)

    to_col(sx, rx, px_s, px_r, False)

    rx[c] = sx[c]

    kk = lax.broadcasted_iota(jnp.int32, (128, 128), 0)
    ll = lax.broadcasted_iota(jnp.int32, (128, 128), 1)
    kl = kk - jnp.where(ll >= 64, 64, 0)
    for n in range(2 * N):
        at = slice(n * 128, n * 128 + 128)
        sel[0, :, at] = jnp.where(kl == 32 + n, 1.0, 0.0).astype(BF16)
        sel[1, :, at] = jnp.where(kk == 32 + n, 1.0, 0.0).astype(BF16)
        sel[2, :, at] = jnp.where(kk == 96 + n, 1.0, 0.0).astype(BF16)

    for load in loads[3:]:
        load.wait()
    ea = lax.broadcasted_iota(jnp.int32, (64, 128), 0)
    eb = lax.broadcasted_iota(jnp.int32, (64, 128), 1)
    wd_ref[...] = jnp.zeros((128, 384), BF16)
    wd_ref[0:32, 0:128] = dot(wdtr[0], jnp.where(ea == eb, 1.0, 0.0).astype(BF16)).astype(BF16)
    wd_ref[64:96, 0:128] = dot(wdtr[1], jnp.where(ea == eb - 64, 1.0, 0.0).astype(BF16)).astype(BF16)
    wd_ref[0:32, 128:256] = wdtc[0]
    wd_ref[64:96, 256:384] = wdtc[1]

    def beside(a, b):
        return jnp.concatenate([a, b], axis=1)

    bias_row = beside(biasr[0:1, :], biasr[1:2, :])
    skip = beside(skipr[...], skipr[...])
    conv_bias = beside(biask[...], biask[...])
    taps = [[beside(kern[i, j : j + 1, :], kern[i, 2 - j : 3 - j, :]) for j in range(3)] for i in range(3)]
    rate_all = beside(rater[0], rater[1]) * -LOG2E

    base = jnp.where(c < half, c, C - 1 - c)

    @pl.loop(0, half)
    def _(k):
        b = lax.rem(base + k, half)
        o = C - 1 - b
        for s in (b, o):
            @pl.when(s != c)
            def _():
                col_copy(rp, rp, pp_s.at[s], pp_r.at[s], s, s, s).wait_recv()
        pb, po = rp[b].astype(F32), rp[o].astype(F32)
        for at, mine, other in ((b, pb, po), (o, po, pb)):
            src = jnp.where(low, mine, turn(other)).astype(BF16)
            rows = pl.ds(pl.multiple_of(at * 64, 64), 64)
            step[rows, :] = softplus(dot(src, wd_ref[:, 0:128]) + bias_row)
            for q in range(8):
                bc[rows, q * 512 : q * 512 + 512] = dot(src, sel[0, :, q * 512 : q * 512 + 512])

    @pl.loop(0, half)
    def _(k):
        b = lax.rem(base + k, half)
        o = C - 1 - b
        for s in (b, o):
            @pl.when(s != c)
            def _():
                col_copy(sx, rx, px_s.at[s], px_r.at[s], s, s, s).wait_recv()
        vb, vo = rx[b].astype(F32), rx[o].astype(F32)
        tb_, to_ = turn(vb), turn(vo)
        brow, orow = pl.ds(pl.multiple_of(b * 64, 64), 64), pl.ds(pl.multiple_of(o * 64, 64), 64)
        x2[brow, :] = jnp.where(low, vb, swap(to_))
        x2[orow, :] = jnp.where(low, vo, swap(tb_))
        sg[brow, :] = silu(jnp.where(low, swap(vb), to_))

    rates = [rate_all[n : n + 1, :] for n in range(N)]
    zero_states = tuple(jnp.zeros((8, 128), F32) for _ in range(N))

    def put(row, out):
        y2[pl.ds(row, 8), :] = out

    def row_body(i, states):
        rows = [pl.multiple_of(i * 64 + 8 * u, 8) for u in range(8)]
        return scan_block(states, rows, step, x2, bc, rows, rates, put)

    lax.fori_loop(0, C, row_body, zero_states)

    z[0:8, :] = jnp.zeros((8, 128), F32)
    for b in range(half):
        here, there = slice(64 * b, 64 * b + 64), slice(64 * (C - 1 - b), 64 * (C - b))
        mix = skip * x2[here, :] + y2[here, :] + swap(turn(y2[there, :]))
        gated = (mix * sg[here, :]).astype(BF16).astype(F32)
        z[64 * b + 8 : 64 * b + 72, :] = gated
    z[8 * TW + 8 : 8 * TW + 16, :] = swap(z[8 * TW : 8 * TW + 8, :])

    sh[0] = z[pl.ds(8 + 7, TW, stride=8), :].astype(BF16)
    sh[1] = z[pl.ds(8, TW, stride=8), :].astype(BF16)
    down = row_copy(sh, rh, h_s.at[0], h_r.at[0], 0, 0, lax.rem(r + 1, R))
    up = row_copy(sh, rh, h_s.at[1], h_r.at[1], 1, 1, lax.rem(r + R - 1, R))

    @pl.when(r < R - 1)
    def _():
        down.start()

    @pl.when(r > 0)
    def _():
        up.start()

    @sent.append
    def _():
        @pl.when(r < R - 1)
        def _():
            down.wait_send()

        @pl.when(r > 0)
        def _():
            up.wait_send()

    sub = lax.broadcasted_iota(jnp.int32, (8, 128), 0)

    @pl.loop(0, half)
    def _(b):
        group = [z[pl.ds(pl.multiple_of(b * 64 + 8 * u, 8), 8), :] for u in range(10)]
        for u in range(8):
            q = [taps[i][0] * group[u] + taps[i][1] * group[u + 1] + taps[i][2] * group[u + 2]
                 for i in range(3)]
            above = jnp.where(sub == 0, 0.0, pltpu.roll(q[0], 1, 0))
            below = jnp.where(sub == 7, 0.0, pltpu.roll(q[2], 7, 0))
            acc[pl.ds(pl.multiple_of(b * 64 + 8 * u, 8), 8), :] = conv_bias + above + q[1] + below

    @pl.when(r == 0)
    def _():
        rh[0] = jnp.zeros((TW, 128), BF16)

    @pl.when(r == R - 1)
    def _():
        rh[1] = jnp.zeros((TW, 128), BF16)

    @pl.when(r > 0)
    def _():
        down.wait_recv()

    @pl.when(r < R - 1)
    def _():
        up.wait_recv()

    for side, i, first in ((0, 0, 0), (1, 2, 7)):
        hz[0:8, :] = jnp.zeros((8, 128), F32)
        halo = rh[side].astype(F32)
        hz[8 : 8 + TW, :] = halo
        hz[8 + TW : 16 + TW, :] = swap(jnp.broadcast_to(halo[TW - 1 : TW, :], (8, 128)))
        add = (taps[i][0] * hz[7 : 7 + TW, :] + taps[i][1] * halo + taps[i][2] * hz[9 : 9 + TW, :])
        at = pl.ds(first, TW, stride=8)
        acc[at, :] = acc[at, :] + add

    for b in range(half):
        cells = silu(acc[64 * b : 64 * b + 64, :]).astype(BF16).astype(F32)
        near, far = cells[0:32, :], swap(turn(cells[32:64, :]))
        s3[b] = jnp.where(low, near, far).astype(BF16)
        s3[C - 1 - b] = jnp.where(low, far, near).astype(BF16)

    to_col(s3, r3, m_s, m_r, False)

    r3[c] = s3[c]

    @pl.loop(0, C)
    def _(s):
        @pl.when(s != c)
        def _():
            col_copy(s3, r3, m_s.at[s], m_r.at[s], s, s, s).wait_recv()

    total = jnp.zeros((64, 128), F32)
    for j in range(R):
        one, two = r3[2 * j].astype(F32), r3[2 * j + 1].astype(F32)
        first = jnp.where(low, one, swap(two))
        second = jnp.where(low, swap(one), two)
        tokens = jnp.concatenate([first, turn(second)], axis=0).astype(BF16)
        tokens = dot(perm, tokens).astype(BF16)
        s4[j] = tokens
        total = total + dot(tokens, wcp_ref[128 * j : 128 * j + 128, :])
    rp4[r] = total.astype(BF16)

    to_row(rp4, rp4, q_s, q_r, True)

    to_row(s4, r4, c_s, c_r, False)

    r4[r] = s4[r]

    HT = 64 * R

    @pl.loop(0, R)
    def _(k):
        s = lax.rem(r + k, R)

        @pl.when(s != r)
        def _():
            row_copy(rp4, rp4, q_s.at[s], q_r.at[s], s, s, s).wait_recv()

        src = rp4[s]
        for d in range(2):
            rows = pl.ds(pl.multiple_of(d * HT + s * 64, 64), 64)
            raw = dot(src, wd_ref[:, 128 + 128 * d : 256 + 128 * d])
            step[rows, :] = softplus(raw + biasc[d : d + 1, :])
            for q in range(8):
                bc[rows, q * 512 : q * 512 + 512] = dot(src, sel[1 + d, :, q * 512 : q * 512 + 512])

    @pl.loop(0, R)
    def _(k):
        s = lax.rem(r + k, R)

        @pl.when(s != r)
        def _():
            row_copy(s4, r4, c_s.at[s], c_r.at[s], s, s, s).wait_recv()

        cells = r4[s].astype(F32)
        for d in range(2):
            x2[pl.ds(pl.multiple_of(d * HT + s * 64, 64), 64), :] = cells

    for d in range(2):
        rate_d = ratec[d] * -LOG2E
        rates_d = [rate_d[n : n + 1, :] for n in range(N)]

        def col_body(i, states):
            block = i if d == 0 else R - 1 - i
            order = range(8) if d == 0 else range(7, -1, -1)
            rows = [pl.multiple_of(d * HT + block * 64 + 8 * u, 8) for u in order]
            return scan_block(states, rows, step, x2, bc, rows, rates_d, put)

        lax.fori_loop(0, R, col_body, zero_states)

    for b in range(R):
        out_ref[64 * b : 64 * b + 64, :] = (
            y2[64 * b : 64 * b + 64, :] + y2[HT + 64 * b : HT + 64 * b + 64, :]).astype(BF16)

    finish()


def local(R, C, features, gate_branch, w_row_proj, w_dt_row, dt_bias_row, rate_row, skip_row,
          conv_kernel, conv_bias, w_col_proj, w_dt_col, dt_bias_col, rate_col):
    E = features.shape[2]
    dma = pltpu.SemaphoreType.DMA
    TW = 4 * C
    out = pl.pallas_call(
        functools.partial(kernel, R, C),
        out_shape=jax.ShapeDtypeStruct((64 * R, 128), BF16),
        in_specs=[pl.BlockSpec(memory_space=pltpu.HBM)] * 13,
        out_specs=pl.BlockSpec(memory_space=pltpu.VMEM),
        scratch_shapes=[
            pltpu.VMEM((64, E), BF16),
            pltpu.VMEM((64, E), BF16),
            pltpu.VMEM((E, 128), BF16),
            pltpu.VMEM((2, 32, 64), BF16),
            pltpu.VMEM((2, 64), F32),
            pltpu.VMEM((2, N, 64), F32),
            pltpu.VMEM((1, 64), F32),
            pltpu.VMEM((3, 3, 64), F32),
            pltpu.VMEM((1, 64), F32),
            pltpu.VMEM((E, 128), BF16),
            pltpu.VMEM((2, 32, 128), BF16),
            pltpu.VMEM((2, 128), F32),
            pltpu.VMEM((2, N, 128), F32),
            pltpu.VMEM((128, 384), BF16),
            dma((13,)),
            pltpu.VMEM((C, 64, 128), BF16),
            pltpu.VMEM((C, 64, 128), BF16),
            pltpu.VMEM((C, 64, 128), BF16),
            pltpu.VMEM((2, TW, 128), BF16),
            pltpu.VMEM((2, TW, 128), BF16),
            pltpu.VMEM((C, 32, 128), BF16),
            pltpu.VMEM((C, 32, 128), BF16),
            pltpu.VMEM((R, 64, 128), BF16),
            pltpu.VMEM((R, 64, 128), BF16),
            pltpu.VMEM((R, 64, 128), BF16),
            pltpu.VMEM((3, 128, 4096), BF16),
            pltpu.VMEM((64 * C, 4096), F32),
            pltpu.VMEM((64 * C, 128), F32),
            pltpu.VMEM((64 * C, 128), F32),
            pltpu.VMEM((64 * C, 128), F32),
            pltpu.VMEM((32 * C, 128), F32),
            pltpu.VMEM((32 * C + 16, 128), F32),
            pltpu.VMEM((32 * C, 128), F32),
            pltpu.VMEM((TW + 16, 128), F32),
            dma((C,)), dma((C,)), dma((C,)), dma((C,)), dma((2,)), dma((2,)),
            dma((C,)), dma((C,)), dma((R,)), dma((R,)), dma((R,)), dma((R,)),
        ],
        compiler_params=pltpu.CompilerParams(
            collective_id=0, has_side_effects=True, vmem_limit_bytes=63 << 20),
    )(features.reshape(64, E), gate_branch.reshape(64, E), w_row_proj, w_dt_row, dt_bias_row,
      jnp.transpose(rate_row, (0, 2, 1)), skip_row.reshape(1, 64), conv_kernel,
      conv_bias.reshape(1, 64), w_col_proj, w_dt_col, dt_bias_col, jnp.transpose(rate_col, (0, 2, 1)))
    return out.reshape(8 * R, 8, 128)


def solution(mesh):
    return jax.shard_map(
        functools.partial(local, mesh.shape["row"], mesh.shape["col"]),
        mesh=mesh,
        in_specs=(
            P("row", "col", None),
            P("row", "col", None),
            P(),
            P(None, None, "col"),
            P(None, "col"),
            P(None, "col", None),
            P("col"),
            P(None, None, "col"),
            P("col"),
            P(),
            P(None, None, "row"),
            P(None, "row"),
            P(None, "row", None),
        ),
        out_specs=P(None, "col", "row"),
        check_vma=False,
    )
```

```python
import functools

import jax
import jax.numpy as jnp
from jax import lax
from jax.experimental import pallas as pl
from jax.experimental.pallas import tpu as pltpu
from jax.sharding import PartitionSpec as P

F32, BF16 = jnp.float32, jnp.bfloat16
MESH = pl.DeviceIdType.MESH
N = 16
LOG2E = 1.4426950408889634


def softplus(v):
    return jnp.maximum(v, 0.0) + jnp.log1p(jnp.exp(-jnp.abs(v)))


def silu(v):
    return v / (1.0 + jnp.exp(-v))


def turn(v):
    groups = v.shape[0] // 8
    return jnp.concatenate([v[8 * g : 8 * g + 8] for g in reversed(range(groups))], axis=0)


def swap(v):
    return pltpu.roll(v, 64, 1)


def dot(a, b):
    return jnp.dot(a, b, preferred_element_type=F32)


def scan_block(states, rows, x_rows, step_ref, x_ref, bc_ref, rates, emit):
    states = list(states)
    for row, x_row in zip(rows, x_rows):
        step = step_ref[pl.ds(row, 8), :]
        drive = step * x_ref[pl.ds(x_row, 8), :]
        out = None
        for n in range(N):
            decay = jnp.exp2(step * rates[n])
            states[n] = decay * states[n] + drive * bc_ref[pl.ds(row, 8), n * 128 : (n + 1) * 128]
            term = states[n] * bc_ref[pl.ds(row, 8), (N + n) * 128 : (N + n + 1) * 128]
            out = term if out is None else out + term
        emit(row, out)
    return tuple(states)


def kernel(
    R, C,
    f_hbm, g_hbm, wrp_hbm, wdtr_hbm, biasr_hbm, rater_hbm, skip_hbm, kern_hbm, biask_hbm, wcp_hbm,
    wdtc_hbm, biasc_hbm, ratec_hbm,
    out_ref,
    f_ref, g_ref, wrp_ref, wdtr, biasr, rater, skipr, kern, biask, wcp_ref, wdtc, biasc, ratec,
    wd_ref, load_sem,
    sx, rx, rp, sh, rh, s3, r3, tok, s4, r4, rp4,
    sel, bc, step, x2, y2, sg, z, acc, hz,
    px_s, px_r, pp_s, pp_r, h_s, h_r, m_s, m_r, c_s, c_r, q_s, q_r,
):
    r, c = lax.axis_index("row"), lax.axis_index("col")
    half = C // 2
    TW = half * 8
    lane = lax.broadcasted_iota(jnp.int32, (1, 128), 1)
    low = lane < 64

    def col_copy(src, dst, ss, rs, slot_src, slot_dst, to):
        return pltpu.make_async_remote_copy(
            src_ref=src.at[slot_src], dst_ref=dst.at[slot_dst], send_sem=ss, recv_sem=rs,
            device_id={"col": to}, device_id_type=MESH)

    def row_copy(src, dst, ss, rs, slot_src, slot_dst, to):
        return pltpu.make_async_remote_copy(
            src_ref=src.at[slot_src], dst_ref=dst.at[slot_dst], send_sem=ss, recv_sem=rs,
            device_id={"row": to}, device_id_type=MESH)

    def send(axis, src, dst, ss, rs, own):
        me, size = (c, C) if axis == "col" else (r, R)
        for k in range(1, size):
            to = lax.rem(me + k, size)
            pltpu.make_async_remote_copy(
                src_ref=src.at[me if own else to], dst_ref=dst.at[me], send_sem=ss, recv_sem=rs,
                device_id={axis: to}, device_id_type=MESH).start()

    def every(axis, ref, ss, rs):
        me, size = (c, C) if axis == "col" else (r, R)
        some = ref.at[pl.ds(0, size - 1)]
        return pltpu.make_async_remote_copy(
            src_ref=some, dst_ref=some, send_sem=ss, recv_sem=rs,
            device_id={axis: lax.rem(me + 1, size)}, device_id_type=MESH)

    sources = (f_hbm, wrp_hbm, g_hbm, wdtr_hbm, biasr_hbm, rater_hbm, skip_hbm, kern_hbm, biask_hbm,
               wcp_hbm, wdtc_hbm, biasc_hbm, ratec_hbm)
    targets = (f_ref, wrp_ref, g_ref, wdtr, biasr, rater, skipr, kern, biask,
               wcp_ref, wdtc, biasc, ratec)
    loads = [pltpu.make_async_copy(a, b, load_sem.at[i])
             for i, (a, b) in enumerate(zip(sources, targets))]
    for load in loads[:3]:
        load.start()

    barrier = pltpu.get_barrier_semaphore()
    for k in range(1, C):
        pl.semaphore_signal(barrier, inc=1, device_id={"col": lax.rem(c + k, C)}, device_id_type=MESH)
    for k in range(1, R):
        pl.semaphore_signal(barrier, inc=1, device_id={"row": lax.rem(r + k, R)}, device_id_type=MESH)

    for load in loads[3:]:
        load.start()

    ta = lax.broadcasted_iota(jnp.int32, (64, 64), 0)
    tb = lax.broadcasted_iota(jnp.int32, (64, 64), 1)
    perm = jnp.where(tb == lax.rem(ta, 8) * 8 + lax.div(ta, 8), 1.0, 0.0).astype(BF16)

    loads[0].wait()
    loads[1].wait()
    proj = dot(f_ref[...], wrp_ref[...]).astype(BF16)
    rp[c] = dot(perm, proj).astype(BF16)

    loads[2].wait()
    for j in range(half):
        fj = dot(perm, f_ref[:, 128 * j : 128 * j + 128])
        gj = dot(perm, g_ref[:, 128 * j : 128 * j + 128])
        sx[2 * j] = jnp.where(low, fj, swap(gj)).astype(BF16)
        sx[2 * j + 1] = jnp.where(low, swap(fj), gj).astype(BF16)

    pl.semaphore_wait(barrier, C - 1 + R - 1)
    for k in range(1, C):
        to = lax.rem(c + k, C)
        col_copy(rp, rp, pp_s, pp_r.at[c], c, c, to).start()
    send("col", sx, rx, px_s, px_r, False)
    rx[c] = sx[c]

    kk = lax.broadcasted_iota(jnp.int32, (128, 128), 0)
    ll = lax.broadcasted_iota(jnp.int32, (128, 128), 1)
    kl = kk - jnp.where(ll >= 64, 64, 0)
    for n in range(2 * N):
        at = slice(n * 128, n * 128 + 128)
        sel[0, :, at] = jnp.where(kl == 32 + n, 1.0, 0.0).astype(BF16)
        sel[1, :, at] = jnp.where(kk == 32 + n, 1.0, 0.0).astype(BF16)
        sel[2, :, at] = jnp.where(kk == 96 + n, 1.0, 0.0).astype(BF16)

    for load in loads[3:]:
        load.wait()
    ea = lax.broadcasted_iota(jnp.int32, (64, 128), 0)
    eb = lax.broadcasted_iota(jnp.int32, (64, 128), 1)
    wd_ref[...] = jnp.zeros((128, 384), BF16)
    wd_ref[0:32, 0:128] = dot(wdtr[0], jnp.where(ea == eb, 1.0, 0.0).astype(BF16)).astype(BF16)
    wd_ref[64:96, 0:128] = dot(wdtr[1], jnp.where(ea == eb - 64, 1.0, 0.0).astype(BF16)).astype(BF16)
    wd_ref[0:32, 128:256] = wdtc[0]
    wd_ref[64:96, 256:384] = wdtc[1]

    def beside(a, b):
        return jnp.concatenate([a, b], axis=1)

    bias_row = beside(biasr[0:1, :], biasr[1:2, :])
    skip = beside(skipr[...], skipr[...])
    conv_bias = beside(biask[...], biask[...])
    taps = [[beside(kern[i, j : j + 1, :], kern[i, 2 - j : 3 - j, :]) for j in range(3)] for i in range(3)]
    rate_all = beside(rater[0], rater[1]) * -LOG2E

    base = jnp.where(c < half, c, C - 1 - c)
    first = lax.div(base, 2)

    @pl.loop(0, half // 2)
    def _(k):
        b = lax.rem(first + k, half // 2) * 2
        blocks = (b, b + 1, C - 2 - b, C - 1 - b)
        for s in blocks:
            @pl.when(s != c)
            def _():
                col_copy(rp, rp, pp_s, pp_r.at[s], s, s, s).wait_recv()
        projs = [rp[s].astype(F32) for s in blocks]
        src = jnp.concatenate(
            [jnp.where(low, projs[i], turn(projs[3 - i])) for i in range(4)], axis=0).astype(BF16)
        rows = [pl.ds(pl.multiple_of(s * 64, 64), 64) for s in blocks]
        steps = softplus(dot(src, wd_ref[:, 0:128]) + bias_row)
        for i in range(4):
            step[rows[i], :] = steps[64 * i : 64 * i + 64, :]
        for q in range(8):
            spread = dot(src, sel[0, :, q * 512 : q * 512 + 512])
            for i in range(4):
                bc[rows[i], q * 512 : q * 512 + 512] = spread[64 * i : 64 * i + 64, :]

    every("col", rx, px_s, px_r).wait_recv()
    for b in range(half):
        o = C - 1 - b
        vb, vo = rx[b].astype(F32), rx[o].astype(F32)
        tb_, to_ = turn(vb), turn(vo)
        x2[64 * b : 64 * b + 64, :] = jnp.where(low, vb, swap(to_))
        x2[64 * o : 64 * o + 64, :] = jnp.where(low, vo, swap(tb_))
        sg[64 * b : 64 * b + 64, :] = silu(jnp.where(low, swap(vb), to_))

    rates = [rate_all[n : n + 1, :] for n in range(N)]
    zero_states = tuple(jnp.zeros((8, 128), F32) for _ in range(N))

    def put(row, out):
        y2[pl.ds(row, 8), :] = out

    def row_body(i, states):
        rows = [pl.multiple_of(i * 64 + 8 * u, 8) for u in range(8)]
        return scan_block(states, rows, rows, step, x2, bc, rates, put)

    lax.fori_loop(0, C, row_body, zero_states)

    z[0:8, :] = jnp.zeros((8, 128), F32)
    for b in range(half):
        here, there = slice(64 * b, 64 * b + 64), slice(64 * (C - 1 - b), 64 * (C - b))
        mix = skip * x2[here, :] + y2[here, :] + swap(turn(y2[there, :]))
        gated = (mix * sg[here, :]).astype(BF16).astype(F32)
        z[64 * b + 8 : 64 * b + 72, :] = gated
    z[8 * TW + 8 : 8 * TW + 16, :] = swap(z[8 * TW : 8 * TW + 8, :])

    sh[0] = z[pl.ds(8 + 7, TW, stride=8), :].astype(BF16)
    sh[1] = z[pl.ds(8, TW, stride=8), :].astype(BF16)
    down = row_copy(sh, rh, h_s.at[0], h_r.at[0], 0, 0, lax.rem(r + 1, R))
    up = row_copy(sh, rh, h_s.at[1], h_r.at[1], 1, 1, lax.rem(r + R - 1, R))

    @pl.when(r < R - 1)
    def _():
        down.start()

    @pl.when(r > 0)
    def _():
        up.start()

    sub = lax.broadcasted_iota(jnp.int32, (8, 128), 0)

    @pl.loop(0, half)
    def _(b):
        group = [z[pl.ds(pl.multiple_of(b * 64 + 8 * u, 8), 8), :] for u in range(10)]
        for u in range(8):
            q = [taps[i][0] * group[u] + taps[i][1] * group[u + 1] + taps[i][2] * group[u + 2]
                 for i in range(3)]
            above = jnp.where(sub == 0, 0.0, pltpu.roll(q[0], 1, 0))
            below = jnp.where(sub == 7, 0.0, pltpu.roll(q[2], 7, 0))
            acc[pl.ds(pl.multiple_of(b * 64 + 8 * u, 8), 8), :] = conv_bias + above + q[1] + below

    every("col", sx, pp_s, px_r).wait_send()
    every("col", sx, px_s, px_r).wait_send()
    @pl.when(r == 0)
    def _():
        rh[0] = jnp.zeros((TW, 128), BF16)

    @pl.when(r == R - 1)
    def _():
        rh[1] = jnp.zeros((TW, 128), BF16)

    @pl.when(r > 0)
    def _():
        down.wait_recv()

    @pl.when(r < R - 1)
    def _():
        up.wait_recv()

    for side, i, first in ((0, 0, 0), (1, 2, 7)):
        hz[0:8, :] = jnp.zeros((8, 128), F32)
        halo = rh[side].astype(F32)
        hz[8 : 8 + TW, :] = halo
        hz[8 + TW : 16 + TW, :] = swap(jnp.broadcast_to(halo[TW - 1 : TW, :], (8, 128)))
        add = (taps[i][0] * hz[7 : 7 + TW, :] + taps[i][1] * halo + taps[i][2] * hz[9 : 9 + TW, :])
        at = pl.ds(first, TW, stride=8)
        acc[at, :] = acc[at, :] + add

    for b in range(half):
        cells = silu(acc[64 * b : 64 * b + 64, :]).astype(BF16).astype(F32)
        near, far = cells[0:32, :], swap(turn(cells[32:64, :]))
        s3[b] = jnp.where(low, near, far).astype(BF16)
        s3[C - 1 - b] = jnp.where(low, far, near).astype(BF16)

    send("col", s3, r3, m_s, m_r, False)
    r3[c] = s3[c]
    every("col", r3, m_s, m_r).wait_recv()

    for j in range(R):
        one, two = r3[2 * j].astype(F32), r3[2 * j + 1].astype(F32)
        tok[0:32, 128 * j : 128 * j + 128] = jnp.where(low, one, swap(two)).astype(BF16)
        tok[32:64, 128 * j : 128 * j + 128] = turn(jnp.where(low, swap(one), two)).astype(BF16)
    rp4[r] = dot(perm, dot(tok[...], wcp_ref[...]).astype(BF16)).astype(BF16)
    send("row", rp4, rp4, q_s, q_r, True)
    for j in range(R):
        s4[j] = dot(perm, tok[:, 128 * j : 128 * j + 128]).astype(BF16)
    send("row", s4, r4, c_s, c_r, False)
    r4[r] = s4[r]
    every("col", s3, m_s, m_r).wait_send()

    @pl.when(r < R - 1)
    def _():
        down.wait_send()

    @pl.when(r > 0)
    def _():
        up.wait_send()

    HT = 64 * R

    every("row", rp4, q_s, q_r).wait_recv()
    src4 = rp4[...].reshape(HT, 128)
    for d in range(2):
        raw = dot(src4, wd_ref[:, 128 + 128 * d : 256 + 128 * d])
        step[d * HT : d * HT + HT, :] = softplus(raw + biasc[d : d + 1, :])

    @pl.loop(0, 8)
    def _(q):
        at = pl.ds(pl.multiple_of(q * 512, 512), 512)
        for d in range(2):
            bc[d * HT : d * HT + HT, at] = dot(rp4[...].reshape(HT, 128), sel[1 + d, :, at])

    every("row", r4, c_s, c_r).wait_recv()
    x2[0:HT, :] = r4[...].reshape(HT, 128).astype(F32)

    for d in range(2):
        rate_d = ratec[d] * -LOG2E
        rates_d = [rate_d[n : n + 1, :] for n in range(N)]

        def col_body(i, states):
            block = i if d == 0 else R - 1 - i
            order = range(8) if d == 0 else range(7, -1, -1)
            rows = [pl.multiple_of(d * HT + block * 64 + 8 * u, 8) for u in order]
            x_rows = [pl.multiple_of(block * 64 + 8 * u, 8) for u in order]
            return scan_block(states, rows, x_rows, step, x2, bc, rates_d, put)

        lax.fori_loop(0, R, col_body, zero_states)

    for b in range(R):
        out_ref[64 * b : 64 * b + 64, :] = (
            y2[64 * b : 64 * b + 64, :] + y2[HT + 64 * b : HT + 64 * b + 64, :]).astype(BF16)

    every("row", s4, q_s, q_r).wait_send()
    every("row", s4, c_s, c_r).wait_send()


def local(R, C, features, gate_branch, w_row_proj, w_dt_row, dt_bias_row, rate_row, skip_row,
          conv_kernel, conv_bias, w_col_proj, w_dt_col, dt_bias_col, rate_col):
    E = features.shape[2]
    dma = pltpu.SemaphoreType.DMA
    TW = 4 * C
    out = pl.pallas_call(
        functools.partial(kernel, R, C),
        out_shape=jax.ShapeDtypeStruct((64 * R, 128), BF16),
        in_specs=[pl.BlockSpec(memory_space=pltpu.HBM)] * 13,
        out_specs=pl.BlockSpec(memory_space=pltpu.VMEM),
        scratch_shapes=[
            pltpu.VMEM((64, E), BF16),
            pltpu.VMEM((64, E), BF16),
            pltpu.VMEM((E, 128), BF16),
            pltpu.VMEM((2, 32, 64), BF16),
            pltpu.VMEM((2, 64), F32),
            pltpu.VMEM((2, N, 64), F32),
            pltpu.VMEM((1, 64), F32),
            pltpu.VMEM((3, 3, 64), F32),
            pltpu.VMEM((1, 64), F32),
            pltpu.VMEM((E, 128), BF16),
            pltpu.VMEM((2, 32, 128), BF16),
            pltpu.VMEM((2, 128), F32),
            pltpu.VMEM((2, N, 128), F32),
            pltpu.VMEM((128, 384), BF16),
            dma((13,)),
            pltpu.VMEM((C, 64, 128), BF16),
            pltpu.VMEM((C, 64, 128), BF16),
            pltpu.VMEM((C, 64, 128), BF16),
            pltpu.VMEM((2, TW, 128), BF16),
            pltpu.VMEM((2, TW, 128), BF16),
            pltpu.VMEM((C, 32, 128), BF16),
            pltpu.VMEM((C, 32, 128), BF16),
            pltpu.VMEM((64, E), BF16),
            pltpu.VMEM((R, 64, 128), BF16),
            pltpu.VMEM((R, 64, 128), BF16),
            pltpu.VMEM((R, 64, 128), BF16),
            pltpu.VMEM((3, 128, 4096), BF16),
            pltpu.VMEM((64 * C, 4096), F32),
            pltpu.VMEM((64 * C, 128), F32),
            pltpu.VMEM((64 * C, 128), F32),
            pltpu.VMEM((64 * C, 128), F32),
            pltpu.VMEM((32 * C, 128), F32),
            pltpu.VMEM((32 * C + 16, 128), F32),
            pltpu.VMEM((32 * C, 128), F32),
            pltpu.VMEM((TW + 16, 128), F32),
            dma, dma, dma, dma((C,)), dma((2,)), dma((2,)), dma, dma, dma, dma, dma, dma,
        ],
        compiler_params=pltpu.CompilerParams(
            collective_id=0, has_side_effects=True, vmem_limit_bytes=40 << 20),
    )(*(pltpu.with_memory_space_constraint(v, pltpu.HBM) for v in (
        features.reshape(64, E), gate_branch.reshape(64, E), w_row_proj, w_dt_row, dt_bias_row,
        jnp.transpose(rate_row, (0, 2, 1)), skip_row.reshape(1, 64), conv_kernel,
        conv_bias.reshape(1, 64), w_col_proj, w_dt_col, dt_bias_col,
        jnp.transpose(rate_col, (0, 2, 1)))))
    return out.reshape(8 * R, 8, 128)


def solution(mesh):
    return jax.shard_map(
        functools.partial(local, mesh.shape["row"], mesh.shape["col"]),
        mesh=mesh,
        in_specs=(
            P("row", "col", None),
            P("row", "col", None),
            P(),
            P(None, None, "col"),
            P(None, "col"),
            P(None, "col", None),
            P("col"),
            P(None, None, "col"),
            P("col"),
            P(),
            P(None, None, "row"),
            P(None, "row"),
            P(None, "row", None),
        ),
        out_specs=P(None, "col", "row"),
        check_vma=False,
    )
```

```python
import functools

import jax
import jax.numpy as jnp
from jax import lax
from jax.experimental import pallas as pl
from jax.experimental.pallas import tpu as pltpu
from jax.sharding import PartitionSpec as P

F32, BF16 = jnp.float32, jnp.bfloat16
MESH = pl.DeviceIdType.MESH
N = 16
LOG2E = 1.4426950408889634


def softplus(v):
    return jnp.maximum(v, 0.0) + jnp.log1p(jnp.exp(-jnp.abs(v)))


def silu(v):
    return v / (1.0 + jnp.exp(-v))


def turn(v):
    groups = v.shape[0] // 8
    return jnp.concatenate([v[8 * g : 8 * g + 8] for g in reversed(range(groups))], axis=0)


def swap(v):
    return pltpu.roll(v, 64, 1)


def dot(a, b):
    return jnp.dot(a, b, preferred_element_type=F32)


def scan_block(states, rows, x_rows, step_ref, x_ref, bc_ref, rates, emit):
    states = list(states)
    for row, x_row in zip(rows, x_rows):
        step = step_ref[pl.ds(row, 8), :]
        drive = step * x_ref[pl.ds(x_row, 8), :]
        out = None
        for n in range(N):
            decay = jnp.exp2(step * rates[n])
            states[n] = decay * states[n] + drive * bc_ref[pl.ds(row, 8), n * 128 : (n + 1) * 128]
            term = states[n] * bc_ref[pl.ds(row, 8), (N + n) * 128 : (N + n + 1) * 128]
            out = term if out is None else out + term
        emit(row, out)
    return tuple(states)


def kernel(
    R, C,
    f_hbm, g_hbm, wrp_hbm, wdtr_hbm, biasr_hbm, rater_hbm, skip_hbm, kern_hbm, biask_hbm, wcp_hbm,
    wdtc_hbm, biasc_hbm, ratec_hbm,
    out_ref,
    f_ref, g_ref, wrp_ref, wdtr, biasr, rater, skipr, kern, biask, wcp_ref, wdtc, biasc, ratec,
    wd_ref, load_sem,
    sx, rx, sgx, rg, rp, sh, rh, s3, r3, s4, r4, rp4,
    sel, bc, step, x2, y2, lay, z, acc, hz,
    px_s, px_r, pg_s, pg_r, pp_s, pp_r, h_s, h_r, m_s, m_r, c_s, c_r, q_s, q_r,
):
    r, c = lax.axis_index("row"), lax.axis_index("col")
    half = C // 2
    TW = half * 8
    lane = lax.broadcasted_iota(jnp.int32, (1, 128), 1)
    low = lane < 64

    def col_copy(src, dst, ss, rs, slot_src, slot_dst, to):
        return pltpu.make_async_remote_copy(
            src_ref=src.at[slot_src], dst_ref=dst.at[slot_dst], send_sem=ss, recv_sem=rs,
            device_id={"col": to}, device_id_type=MESH)

    def row_copy(src, dst, ss, rs, slot_src, slot_dst, to):
        return pltpu.make_async_remote_copy(
            src_ref=src.at[slot_src], dst_ref=dst.at[slot_dst], send_sem=ss, recv_sem=rs,
            device_id={"row": to}, device_id_type=MESH)

    def send(axis, src, dst, ss, rs, own):
        me, size = (c, C) if axis == "col" else (r, R)
        for k in range(1, size):
            to = lax.rem(me + k, size)
            pltpu.make_async_remote_copy(
                src_ref=src.at[me if own else to], dst_ref=dst.at[me], send_sem=ss, recv_sem=rs,
                device_id={axis: to}, device_id_type=MESH).start()

    def every(axis, ref, ss, rs):
        me, size = (c, C) if axis == "col" else (r, R)
        some = ref.at[pl.ds(0, size - 1)]
        return pltpu.make_async_remote_copy(
            src_ref=some, dst_ref=some, send_sem=ss, recv_sem=rs,
            device_id={axis: lax.rem(me + 1, size)}, device_id_type=MESH)

    sources = (f_hbm, wrp_hbm, g_hbm, wdtr_hbm, biasr_hbm, rater_hbm, skip_hbm, kern_hbm, biask_hbm,
               wcp_hbm, wdtc_hbm, biasc_hbm, ratec_hbm)
    targets = (f_ref, wrp_ref, g_ref, wdtr, biasr, rater, skipr, kern, biask,
               wcp_ref, wdtc, biasc, ratec)
    loads = [pltpu.make_async_copy(a, b, load_sem.at[i])
             for i, (a, b) in enumerate(zip(sources, targets))]
    for load in loads[:3]:
        load.start()

    barrier = pltpu.get_barrier_semaphore()
    for k in range(1, C):
        pl.semaphore_signal(barrier, inc=1, device_id={"col": lax.rem(c + k, C)}, device_id_type=MESH)
    for k in range(1, R):
        pl.semaphore_signal(barrier, inc=1, device_id={"row": lax.rem(r + k, R)}, device_id_type=MESH)

    for load in loads[3:]:
        load.start()

    ta = lax.broadcasted_iota(jnp.int32, (64, 64), 0)
    tb = lax.broadcasted_iota(jnp.int32, (64, 64), 1)
    perm = jnp.where(tb == lax.rem(ta, 8) * 8 + lax.div(ta, 8), 1.0, 0.0).astype(BF16)

    def packed(v):
        near, far = v[0:32, :], turn(v[32:64, :])
        return jnp.where(low, near, swap(far)).astype(BF16), jnp.where(low, swap(near), far).astype(BF16)

    loads[0].wait()
    loads[1].wait()
    proj = dot(f_ref[...], wrp_ref[...]).astype(BF16).astype(F32)
    for h in range(8):
        lay[pl.ds(h, 8, stride=8), :] = proj[8 * h : 8 * h + 8, :]
    rp[c] = lay[...].astype(BF16)
    turned = dot(perm, f_ref[...])
    for j in range(half):
        sx[2 * j], sx[2 * j + 1] = packed(turned[:, 128 * j : 128 * j + 128])

    pl.semaphore_wait(barrier, C - 1 + R - 1)
    for k in range(1, C):
        to = lax.rem(c + k, C)
        col_copy(rp, rp, pp_s, pp_r.at[c], c, c, to).start()
    send("col", sx, rx, px_s, px_r, False)
    loads[2].wait()
    turned = dot(perm, g_ref[...])
    for j in range(half):
        sgx[2 * j], sgx[2 * j + 1] = packed(turned[:, 128 * j : 128 * j + 128])
    send("col", sgx, rg, pg_s, pg_r, False)
    rx[c] = sx[c]
    rg[c] = sgx[c]

    kk = lax.broadcasted_iota(jnp.int32, (128, 128), 0)
    ll = lax.broadcasted_iota(jnp.int32, (128, 128), 1)
    kl = kk - jnp.where(ll >= 64, 64, 0)
    for n in range(2 * N):
        at = slice(n * 128, n * 128 + 128)
        sel[0, :, at] = jnp.where(kl == 32 + n, 1.0, 0.0).astype(BF16)
        sel[1, :, at] = jnp.where(kk == 32 + n, 1.0, 0.0).astype(BF16)
        sel[2, :, at] = jnp.where(kk == 96 + n, 1.0, 0.0).astype(BF16)

    for load in loads[3:]:
        load.wait()
    ea = lax.broadcasted_iota(jnp.int32, (64, 128), 0)
    eb = lax.broadcasted_iota(jnp.int32, (64, 128), 1)
    wd_ref[...] = jnp.zeros((128, 384), BF16)
    wd_ref[0:32, 0:128] = dot(wdtr[0], jnp.where(ea == eb, 1.0, 0.0).astype(BF16)).astype(BF16)
    wd_ref[64:96, 0:128] = dot(wdtr[1], jnp.where(ea == eb - 64, 1.0, 0.0).astype(BF16)).astype(BF16)
    wd_ref[0:32, 128:256] = wdtc[0]
    wd_ref[64:96, 256:384] = wdtc[1]

    def beside(a, b):
        return jnp.concatenate([a, b], axis=1)

    bias_row = beside(biasr[0:1, :], biasr[1:2, :])
    skip = beside(skipr[...], skipr[...])
    conv_bias = beside(biask[...], biask[...])
    taps = [[beside(kern[i, j : j + 1, :], kern[i, 2 - j : 3 - j, :]) for j in range(3)] for i in range(3)]
    rate_all = beside(rater[0], rater[1]) * -LOG2E

    base = jnp.where(c < half, c, C - 1 - c)
    first = lax.div(base, 2)

    @pl.loop(0, half // 2)
    def _(k):
        b = lax.rem(first + k, half // 2) * 2
        blocks = (b, b + 1, C - 2 - b, C - 1 - b)
        for s in blocks:
            @pl.when(s != c)
            def _():
                col_copy(rp, rp, pp_s, pp_r.at[s], s, s, s).wait_recv()
        projs = [rp[s].astype(F32) for s in blocks]
        src = jnp.concatenate(
            [jnp.where(low, projs[i], turn(projs[3 - i])) for i in range(4)], axis=0).astype(BF16)
        rows = [pl.ds(pl.multiple_of(s * 64, 64), 64) for s in blocks]
        steps = softplus(dot(src, wd_ref[:, 0:128]) + bias_row)
        for i in range(4):
            step[rows[i], :] = steps[64 * i : 64 * i + 64, :]
        for q in range(8):
            spread = dot(src, sel[0, :, q * 512 : q * 512 + 512])
            for i in range(4):
                bc[rows[i], q * 512 : q * 512 + 512] = spread[64 * i : 64 * i + 64, :]

    def facing(ref, b):
        one, two = ref[b].astype(F32), ref[C - 1 - b].astype(F32)
        p, q = jnp.where(low, one, two), jnp.where(low, two, one)
        return p, turn(swap(q)), q, turn(swap(p))

    every("col", rx, px_s, px_r).wait_recv()
    for b in range(half):
        o = C - 1 - b
        parts = facing(rx, b)
        x2[64 * b : 64 * b + 32, :], x2[64 * b + 32 : 64 * b + 64, :] = parts[0], parts[1]
        x2[64 * o : 64 * o + 32, :], x2[64 * o + 32 : 64 * o + 64, :] = parts[2], parts[3]

    rates = [rate_all[n : n + 1, :] for n in range(N)]
    zero_states = tuple(jnp.zeros((8, 128), F32) for _ in range(N))

    def put(row, out):
        y2[pl.ds(row, 8), :] = out

    def row_body(i, states):
        rows = [pl.multiple_of(i * 64 + 8 * u, 8) for u in range(8)]
        return scan_block(states, rows, rows, step, x2, bc, rates, put)

    lax.fori_loop(0, C, row_body, zero_states)

    every("col", rg, pg_s, pg_r).wait_recv()
    z[0:8, :] = jnp.zeros((8, 128), F32)
    for b in range(half):
        here, there = slice(64 * b, 64 * b + 64), slice(64 * (C - 1 - b), 64 * (C - b))
        mix = skip * x2[here, :] + y2[here, :] + swap(turn(y2[there, :]))
        gate = jnp.concatenate(facing(rg, b)[:2], axis=0)
        gated = (mix * silu(gate)).astype(BF16).astype(F32)
        z[64 * b + 8 : 64 * b + 72, :] = gated
    z[8 * TW + 8 : 8 * TW + 16, :] = swap(z[8 * TW : 8 * TW + 8, :])

    sh[0] = z[pl.ds(8 + 7, TW, stride=8), :].astype(BF16)
    sh[1] = z[pl.ds(8, TW, stride=8), :].astype(BF16)
    down = row_copy(sh, rh, h_s.at[0], h_r.at[0], 0, 0, lax.rem(r + 1, R))
    up = row_copy(sh, rh, h_s.at[1], h_r.at[1], 1, 1, lax.rem(r + R - 1, R))

    @pl.when(r < R - 1)
    def _():
        down.start()

    @pl.when(r > 0)
    def _():
        up.start()

    sub = lax.broadcasted_iota(jnp.int32, (8, 128), 0)

    @pl.loop(0, half)
    def _(b):
        group = [z[pl.ds(pl.multiple_of(b * 64 + 8 * u, 8), 8), :] for u in range(10)]
        for u in range(8):
            q = [taps[i][0] * group[u] + taps[i][1] * group[u + 1] + taps[i][2] * group[u + 2]
                 for i in range(3)]
            above = jnp.where(sub == 0, 0.0, pltpu.roll(q[0], 1, 0))
            below = jnp.where(sub == 7, 0.0, pltpu.roll(q[2], 7, 0))
            acc[pl.ds(pl.multiple_of(b * 64 + 8 * u, 8), 8), :] = conv_bias + above + q[1] + below

    every("col", rp, pp_s, px_r).wait_send()
    every("col", sx, px_s, px_r).wait_send()
    every("col", sgx, pg_s, pg_r).wait_send()
    @pl.when(r == 0)
    def _():
        rh[0] = jnp.zeros((TW, 128), BF16)

    @pl.when(r == R - 1)
    def _():
        rh[1] = jnp.zeros((TW, 128), BF16)

    @pl.when(r > 0)
    def _():
        down.wait_recv()

    @pl.when(r < R - 1)
    def _():
        up.wait_recv()

    for side, i, first in ((0, 0, 0), (1, 2, 7)):
        hz[0:8, :] = jnp.zeros((8, 128), F32)
        halo = rh[side].astype(F32)
        hz[8 : 8 + TW, :] = halo
        hz[8 + TW : 16 + TW, :] = swap(jnp.broadcast_to(halo[TW - 1 : TW, :], (8, 128)))
        add = (taps[i][0] * hz[7 : 7 + TW, :] + taps[i][1] * halo + taps[i][2] * hz[9 : 9 + TW, :])
        at = pl.ds(first, TW, stride=8)
        acc[at, :] = acc[at, :] + add

    for b in range(half):
        cells = silu(acc[64 * b : 64 * b + 64, :]).astype(BF16).astype(F32)
        near, far = cells[0:32, :], swap(turn(cells[32:64, :]))
        s3[b] = jnp.where(low, near, far).astype(BF16)
        s3[C - 1 - b] = jnp.where(low, far, near).astype(BF16)

    send("col", s3, r3, m_s, m_r, False)
    r3[c] = s3[c]
    every("col", r3, m_s, m_r).wait_recv()

    tokens = []
    for j in range(R):
        one, two = r3[2 * j].astype(F32), r3[2 * j + 1].astype(F32)
        tokens.append(jnp.concatenate(
            [jnp.where(low, one, swap(two)), turn(jnp.where(low, swap(one), two))], axis=0).astype(BF16))
        s4[j] = tokens[j]
    proj = dot(jnp.concatenate(tokens, axis=1), wcp_ref[...]).astype(BF16).astype(F32)
    for w in range(8):
        lay[pl.ds(w, 8, stride=8), :] = proj[8 * w : 8 * w + 8, :]
    rp4[r] = lay[...].astype(BF16)
    send("row", rp4, rp4, q_s, q_r, True)
    send("row", s4, r4, c_s, c_r, False)
    r4[r] = s4[r]
    every("col", s3, m_s, m_r).wait_send()

    @pl.when(r < R - 1)
    def _():
        down.wait_send()

    @pl.when(r > 0)
    def _():
        up.wait_send()

    HT = 64 * R

    every("row", rp4, q_s, q_r).wait_recv()
    src4 = rp4[...].reshape(HT, 128)
    for d in range(2):
        raw = dot(src4, wd_ref[:, 128 + 128 * d : 256 + 128 * d])
        step[d * HT : d * HT + HT, :] = softplus(raw + biasc[d : d + 1, :])

    @pl.loop(0, 8)
    def _(q):
        at = pl.ds(pl.multiple_of(q * 512, 512), 512)
        for d in range(2):
            bc[d * HT : d * HT + HT, at] = dot(rp4[...].reshape(HT, 128), sel[1 + d, :, at])

    every("row", r4, c_s, c_r).wait_recv()
    for s in range(R):
        cells = r4[s].astype(F32)
        for w in range(8):
            x2[pl.ds(64 * s + w, 8, stride=8), :] = cells[8 * w : 8 * w + 8, :]

    for d in range(2):
        rate_d = ratec[d] * -LOG2E
        rates_d = [rate_d[n : n + 1, :] for n in range(N)]

        def col_body(i, states):
            block = i if d == 0 else R - 1 - i
            order = range(8) if d == 0 else range(7, -1, -1)
            rows = [pl.multiple_of(d * HT + block * 64 + 8 * u, 8) for u in order]
            x_rows = [pl.multiple_of(block * 64 + 8 * u, 8) for u in order]
            return scan_block(states, rows, x_rows, step, x2, bc, rates_d, put)

        lax.fori_loop(0, R, col_body, zero_states)

    for b in range(R):
        out_ref[64 * b : 64 * b + 64, :] = (
            y2[64 * b : 64 * b + 64, :] + y2[HT + 64 * b : HT + 64 * b + 64, :]).astype(BF16)

    every("row", s4, q_s, q_r).wait_send()
    every("row", s4, c_s, c_r).wait_send()


def local(R, C, features, gate_branch, w_row_proj, w_dt_row, dt_bias_row, rate_row, skip_row,
          conv_kernel, conv_bias, w_col_proj, w_dt_col, dt_bias_col, rate_col):
    E = features.shape[2]
    dma = pltpu.SemaphoreType.DMA
    TW = 4 * C
    out = pl.pallas_call(
        functools.partial(kernel, R, C),
        out_shape=jax.ShapeDtypeStruct((64 * R, 128), BF16),
        in_specs=[pl.BlockSpec(memory_space=pltpu.HBM)] * 13,
        out_specs=pl.BlockSpec(memory_space=pltpu.VMEM),
        scratch_shapes=[
            pltpu.VMEM((64, E), BF16),
            pltpu.VMEM((64, E), BF16),
            pltpu.VMEM((E, 128), BF16),
            pltpu.VMEM((2, 32, 64), BF16),
            pltpu.VMEM((2, 64), F32),
            pltpu.VMEM((2, N, 64), F32),
            pltpu.VMEM((1, 64), F32),
            pltpu.VMEM((3, 3, 64), F32),
            pltpu.VMEM((1, 64), F32),
            pltpu.VMEM((E, 128), BF16),
            pltpu.VMEM((2, 32, 128), BF16),
            pltpu.VMEM((2, 128), F32),
            pltpu.VMEM((2, N, 128), F32),
            pltpu.VMEM((128, 384), BF16),
            dma((13,)),
            pltpu.VMEM((C, 32, 128), BF16),
            pltpu.VMEM((C, 32, 128), BF16),
            pltpu.VMEM((C, 32, 128), BF16),
            pltpu.VMEM((C, 32, 128), BF16),
            pltpu.VMEM((C, 64, 128), BF16),
            pltpu.VMEM((2, TW, 128), BF16),
            pltpu.VMEM((2, TW, 128), BF16),
            pltpu.VMEM((C, 32, 128), BF16),
            pltpu.VMEM((C, 32, 128), BF16),
            pltpu.VMEM((R, 64, 128), BF16),
            pltpu.VMEM((R, 64, 128), BF16),
            pltpu.VMEM((R, 64, 128), BF16),
            pltpu.VMEM((3, 128, 4096), BF16),
            pltpu.VMEM((64 * C, 4096), F32),
            pltpu.VMEM((64 * C, 128), F32),
            pltpu.VMEM((64 * C, 128), F32),
            pltpu.VMEM((64 * C, 128), F32),
            pltpu.VMEM((64, 128), F32),
            pltpu.VMEM((32 * C + 16, 128), F32),
            pltpu.VMEM((32 * C, 128), F32),
            pltpu.VMEM((TW + 16, 128), F32),
            dma, dma, dma, dma, dma, dma((C,)), dma((2,)), dma((2,)), dma, dma, dma, dma, dma, dma,
        ],
        compiler_params=pltpu.CompilerParams(
            collective_id=0, has_side_effects=True, vmem_limit_bytes=40 << 20),
    )(*(pltpu.with_memory_space_constraint(v, pltpu.HBM) for v in (
        features.reshape(64, E), gate_branch.reshape(64, E), w_row_proj, w_dt_row, dt_bias_row,
        jnp.transpose(rate_row, (0, 2, 1)), skip_row.reshape(1, 64), conv_kernel,
        conv_bias.reshape(1, 64), w_col_proj, w_dt_col, dt_bias_col,
        jnp.transpose(rate_col, (0, 2, 1)))))
    return out.reshape(8 * R, 8, 128)


def solution(mesh):
    return jax.shard_map(
        functools.partial(local, mesh.shape["row"], mesh.shape["col"]),
        mesh=mesh,
        in_specs=(
            P("row", "col", None),
            P("row", "col", None),
            P(),
            P(None, None, "col"),
            P(None, "col"),
            P(None, "col", None),
            P("col"),
            P(None, None, "col"),
            P("col"),
            P(),
            P(None, None, "row"),
            P(None, "row"),
            P(None, "row", None),
        ),
        out_specs=P(None, "col", "row"),
        check_vma=False,
    )
```

```python
import functools

import jax
import jax.numpy as jnp
from jax import lax
from jax.experimental import pallas as pl
from jax.experimental.pallas import tpu as pltpu
from jax.sharding import PartitionSpec as P

F32, BF16 = jnp.float32, jnp.bfloat16
MESH = pl.DeviceIdType.MESH
N = 16
LOG2E = 1.4426950408889634


def softplus(v):
    return jnp.maximum(v, 0.0) + jnp.log1p(jnp.exp(-jnp.abs(v)))


def silu(v):
    return v / (1.0 + jnp.exp(-v))


def turn(v):
    groups = v.shape[0] // 8
    return jnp.concatenate([v[8 * g : 8 * g + 8] for g in reversed(range(groups))], axis=0)


def swap(v):
    return pltpu.roll(v, 64, 1)


def dot(a, b):
    return jnp.dot(a, b, preferred_element_type=F32)


def scan_block(states, rows, x_rows, step_ref, x_ref, bc_ref, rates, emit):
    states = list(states)
    for row, x_row in zip(rows, x_rows):
        step = step_ref[pl.ds(row, 8), :]
        drive = step * x_ref[pl.ds(x_row, 8), :]
        out = None
        for n in range(N):
            decay = jnp.exp2(step * rates[n])
            states[n] = decay * states[n] + drive * bc_ref[pl.ds(row, 8), n * 128 : (n + 1) * 128]
            term = states[n] * bc_ref[pl.ds(row, 8), (N + n) * 128 : (N + n + 1) * 128]
            out = term if out is None else out + term
        emit(row, out)
    return tuple(states)


def kernel(
    R, C,
    f_hbm, g_hbm, wrp_hbm, wdtr_hbm, biasr_hbm, rater_hbm, skip_hbm, kern_hbm, biask_hbm, wcp_hbm,
    wdtc_hbm, biasc_hbm, ratec_hbm,
    out_ref,
    f_ref, g_ref, wrp_ref, wdtr, biasr, rater, skipr, kern, biask, wcp_ref, wdtc, biasc, ratec,
    wd_ref, load_sem,
    sx, rx, sgx, rg, rp, srcs, sh, rh, s3, r3, s4, r4, rp4,
    sel, bc, step, x2, y2, lay, z, acc, hz,
    px_s, px_r, pg_s, pg_r, pp_s, pp_r, pf_s, pf_r, h_s, h_r, m_s, m_r, c_s, c_r, q_s, q_r,
):
    r, c = lax.axis_index("row"), lax.axis_index("col")
    half = C // 2
    chip, core = lax.div(c, 2), lax.rem(c, 2)
    TW = half * 8
    lane = lax.broadcasted_iota(jnp.int32, (1, 128), 1)
    low = lane < 64

    def col_copy(src, dst, ss, rs, slot_src, slot_dst, to):
        return pltpu.make_async_remote_copy(
            src_ref=src.at[slot_src], dst_ref=dst.at[slot_dst], send_sem=ss, recv_sem=rs,
            device_id={"col": to}, device_id_type=MESH)

    def row_copy(src, dst, ss, rs, slot_src, slot_dst, to):
        return pltpu.make_async_remote_copy(
            src_ref=src.at[slot_src], dst_ref=dst.at[slot_dst], send_sem=ss, recv_sem=rs,
            device_id={"row": to}, device_id_type=MESH)

    def send(axis, src, dst, ss, rs, own):
        me, size = (c, C) if axis == "col" else (r, R)
        for k in range(1, size):
            to = lax.rem(me + k, size)
            pltpu.make_async_remote_copy(
                src_ref=src.at[me if own else to], dst_ref=dst.at[me], send_sem=ss, recv_sem=rs,
                device_id={axis: to}, device_id_type=MESH).start()

    def every(axis, ref, ss, rs):
        me, size = (c, C) if axis == "col" else (r, R)
        some = ref.at[pl.ds(0, size - 1)]
        return pltpu.make_async_remote_copy(
            src_ref=some, dst_ref=some, send_sem=ss, recv_sem=rs,
            device_id={axis: lax.rem(me + 1, size)}, device_id_type=MESH)

    sources = (f_hbm, wrp_hbm, g_hbm, wdtr_hbm, biasr_hbm, rater_hbm, skip_hbm, kern_hbm, biask_hbm,
               wcp_hbm, wdtc_hbm, biasc_hbm, ratec_hbm)
    targets = (f_ref, wrp_ref, g_ref, wdtr, biasr, rater, skipr, kern, biask,
               wcp_ref, wdtc, biasc, ratec)
    loads = [pltpu.make_async_copy(a, b, load_sem.at[i])
             for i, (a, b) in enumerate(zip(sources, targets))]
    for load in loads[:3]:
        load.start()

    barrier = pltpu.get_barrier_semaphore()
    for k in range(1, C):
        pl.semaphore_signal(barrier, inc=1, device_id={"col": lax.rem(c + k, C)}, device_id_type=MESH)
    for k in range(1, R):
        pl.semaphore_signal(barrier, inc=1, device_id={"row": lax.rem(r + k, R)}, device_id_type=MESH)

    for load in loads[3:]:
        load.start()

    ta = lax.broadcasted_iota(jnp.int32, (64, 64), 0)
    tb = lax.broadcasted_iota(jnp.int32, (64, 64), 1)
    perm = jnp.where(tb == lax.rem(ta, 8) * 8 + lax.div(ta, 8), 1.0, 0.0).astype(BF16)

    def packed(v):
        near, far = v[0:32, :], turn(v[32:64, :])
        return jnp.where(low, near, swap(far)).astype(BF16), jnp.where(low, swap(near), far).astype(BF16)

    loads[0].wait()
    loads[1].wait()
    proj = dot(f_ref[...], wrp_ref[...]).astype(BF16).astype(F32)
    for h in range(8):
        lay[pl.ds(h, 8, stride=8), :] = proj[8 * h : 8 * h + 8, :]
    rp[core, chip] = lay[...].astype(BF16)
    turned = dot(perm, f_ref[...])
    for j in range(half):
        sx[2 * j], sx[2 * j + 1] = packed(turned[:, 128 * j : 128 * j + 128])

    pl.semaphore_wait(barrier, C - 1 + R - 1)
    for k in range(1, half):
        pltpu.make_async_remote_copy(
            src_ref=rp.at[core, chip], dst_ref=rp.at[core, chip], send_sem=pp_s, recv_sem=pp_r,
            device_id={"col": lax.rem(c + 2 * k, C)}, device_id_type=MESH).start()
    send("col", sx, rx, px_s, px_r, False)
    loads[2].wait()
    turned = dot(perm, g_ref[...])
    for j in range(half):
        sgx[2 * j], sgx[2 * j + 1] = packed(turned[:, 128 * j : 128 * j + 128])
    send("col", sgx, rg, pg_s, pg_r, False)
    rx[c] = sx[c]
    rg[c] = sgx[c]

    kk = lax.broadcasted_iota(jnp.int32, (128, 128), 0)
    ll = lax.broadcasted_iota(jnp.int32, (128, 128), 1)
    kl = kk - jnp.where(ll >= 64, 64, 0)
    for n in range(2 * N):
        at = slice(n * 128, n * 128 + 128)
        sel[0, :, at] = jnp.where(kl == 32 + n, 1.0, 0.0).astype(BF16)
        sel[1, :, at] = jnp.where(kk == 32 + n, 1.0, 0.0).astype(BF16)
        sel[2, :, at] = jnp.where(kk == 96 + n, 1.0, 0.0).astype(BF16)

    for load in loads[3:]:
        load.wait()
    ea = lax.broadcasted_iota(jnp.int32, (64, 128), 0)
    eb = lax.broadcasted_iota(jnp.int32, (64, 128), 1)
    wd_ref[...] = jnp.zeros((128, 384), BF16)
    wd_ref[0:32, 0:128] = dot(wdtr[0], jnp.where(ea == eb, 1.0, 0.0).astype(BF16)).astype(BF16)
    wd_ref[64:96, 0:128] = dot(wdtr[1], jnp.where(ea == eb - 64, 1.0, 0.0).astype(BF16)).astype(BF16)
    wd_ref[0:32, 128:256] = wdtc[0]
    wd_ref[64:96, 256:384] = wdtc[1]

    def beside(a, b):
        return jnp.concatenate([a, b], axis=1)

    bias_row = beside(biasr[0:1, :], biasr[1:2, :])
    skip = beside(skipr[...], skipr[...])
    conv_bias = beside(biask[...], biask[...])
    taps = [[beside(kern[i, j : j + 1, :], kern[i, 2 - j : 3 - j, :]) for j in range(3)] for i in range(3)]
    rate_all = beside(rater[0], rater[1]) * -LOG2E

    direct = rp.at[core, pl.ds(0, half - 1)]
    peers = pltpu.make_async_remote_copy(
        src_ref=direct, dst_ref=direct, send_sem=pp_s, recv_sem=pp_r,
        device_id={"col": c + 1 - 2 * core}, device_id_type=MESH)
    peers.wait_recv()
    passed = pltpu.make_async_remote_copy(
        src_ref=rp.at[core], dst_ref=rp.at[core], send_sem=pf_s, recv_sem=pf_r,
        device_id={"col": c + 1 - 2 * core}, device_id_type=MESH)
    passed.start()
    passed.wait_recv()
    for b in range(half):
        o = C - 1 - b
        pb, po = rp[b % 2, b // 2].astype(F32), rp[o % 2, o // 2].astype(F32)
        srcs[64 * b : 64 * b + 64, :] = jnp.where(low, pb, turn(po)).astype(BF16)
        srcs[64 * o : 64 * o + 64, :] = jnp.where(low, po, turn(pb)).astype(BF16)
    step[...] = softplus(dot(srcs[...], wd_ref[:, 0:128]) + bias_row)

    for q in range(8):
        at = slice(q * 512, q * 512 + 512)
        bc[:, at] = dot(srcs[...], sel[0, :, at])

    def facing(ref, b):
        one, two = ref[b].astype(F32), ref[C - 1 - b].astype(F32)
        p, q = jnp.where(low, one, two), jnp.where(low, two, one)
        return p, turn(swap(q)), q, turn(swap(p))

    every("col", rx, px_s, px_r).wait_recv()
    for b in range(half):
        o = C - 1 - b
        parts = facing(rx, b)
        x2[64 * b : 64 * b + 32, :], x2[64 * b + 32 : 64 * b + 64, :] = parts[0], parts[1]
        x2[64 * o : 64 * o + 32, :], x2[64 * o + 32 : 64 * o + 64, :] = parts[2], parts[3]

    rates = [rate_all[n : n + 1, :] for n in range(N)]
    zero_states = tuple(jnp.zeros((8, 128), F32) for _ in range(N))

    def put(row, out):
        y2[pl.ds(row, 8), :] = out

    def row_body(i, states):
        rows = [pl.multiple_of(i * 128 + 8 * u, 8) for u in range(16)]
        return scan_block(states, rows, rows, step, x2, bc, rates, put)

    lax.fori_loop(0, C // 2, row_body, zero_states)

    every("col", rg, pg_s, pg_r).wait_recv()
    z[0:8, :] = jnp.zeros((8, 128), F32)
    for b in range(half):
        here, there = slice(64 * b, 64 * b + 64), slice(64 * (C - 1 - b), 64 * (C - b))
        mix = skip * x2[here, :] + y2[here, :] + swap(turn(y2[there, :]))
        gate = jnp.concatenate(facing(rg, b)[:2], axis=0)
        gated = (mix * silu(gate)).astype(BF16).astype(F32)
        z[64 * b + 8 : 64 * b + 72, :] = gated
    z[8 * TW + 8 : 8 * TW + 16, :] = swap(z[8 * TW : 8 * TW + 8, :])

    sh[0] = z[pl.ds(8 + 7, TW, stride=8), :].astype(BF16)
    sh[1] = z[pl.ds(8, TW, stride=8), :].astype(BF16)
    down = row_copy(sh, rh, h_s.at[0], h_r.at[0], 0, 0, lax.rem(r + 1, R))
    up = row_copy(sh, rh, h_s.at[1], h_r.at[1], 1, 1, lax.rem(r + R - 1, R))

    @pl.when(r < R - 1)
    def _():
        down.start()

    @pl.when(r > 0)
    def _():
        up.start()

    sub = lax.broadcasted_iota(jnp.int32, (8, 128), 0)

    @pl.loop(0, half)
    def _(b):
        group = [z[pl.ds(pl.multiple_of(b * 64 + 8 * u, 8), 8), :] for u in range(10)]
        for u in range(8):
            q = [taps[i][0] * group[u] + taps[i][1] * group[u + 1] + taps[i][2] * group[u + 2]
                 for i in range(3)]
            above = jnp.where(sub == 0, 0.0, pltpu.roll(q[0], 1, 0))
            below = jnp.where(sub == 7, 0.0, pltpu.roll(q[2], 7, 0))
            acc[pl.ds(pl.multiple_of(b * 64 + 8 * u, 8), 8), :] = conv_bias + above + q[1] + below

    peers.wait_send()
    passed.wait_send()
    every("col", sx, px_s, px_r).wait_send()
    every("col", sgx, pg_s, pg_r).wait_send()
    @pl.when(r == 0)
    def _():
        rh[0] = jnp.zeros((TW, 128), BF16)

    @pl.when(r == R - 1)
    def _():
        rh[1] = jnp.zeros((TW, 128), BF16)

    @pl.when(r > 0)
    def _():
        down.wait_recv()

    @pl.when(r < R - 1)
    def _():
        up.wait_recv()

    for side, i, first in ((0, 0, 0), (1, 2, 7)):
        hz[0:8, :] = jnp.zeros((8, 128), F32)
        halo = rh[side].astype(F32)
        hz[8 : 8 + TW, :] = halo
        hz[8 + TW : 16 + TW, :] = swap(jnp.broadcast_to(halo[TW - 1 : TW, :], (8, 128)))
        add = (taps[i][0] * hz[7 : 7 + TW, :] + taps[i][1] * halo + taps[i][2] * hz[9 : 9 + TW, :])
        at = pl.ds(first, TW, stride=8)
        acc[at, :] = acc[at, :] + add

    for b in range(half):
        cells = silu(acc[64 * b : 64 * b + 64, :]).astype(BF16).astype(F32)
        near, far = cells[0:32, :], swap(turn(cells[32:64, :]))
        s3[b] = jnp.where(low, near, far).astype(BF16)
        s3[C - 1 - b] = jnp.where(low, far, near).astype(BF16)

    send("col", s3, r3, m_s, m_r, False)
    r3[c] = s3[c]
    every("col", r3, m_s, m_r).wait_recv()

    tokens = []
    for j in range(R):
        one, two = r3[2 * j].astype(F32), r3[2 * j + 1].astype(F32)
        tokens.append(jnp.concatenate(
            [jnp.where(low, one, swap(two)), turn(jnp.where(low, swap(one), two))], axis=0).astype(BF16))
        s4[j] = tokens[j]
    proj = dot(jnp.concatenate(tokens, axis=1), wcp_ref[...]).astype(BF16).astype(F32)
    for w in range(8):
        lay[pl.ds(w, 8, stride=8), :] = proj[8 * w : 8 * w + 8, :]
    rp4[r] = lay[...].astype(BF16)
    send("row", rp4, rp4, q_s, q_r, True)
    send("row", s4, r4, c_s, c_r, False)
    r4[r] = s4[r]
    every("col", s3, m_s, m_r).wait_send()

    @pl.when(r < R - 1)
    def _():
        down.wait_send()

    @pl.when(r > 0)
    def _():
        up.wait_send()

    HT = 64 * R

    every("row", rp4, q_s, q_r).wait_recv()
    src4 = rp4[...].reshape(HT, 128)
    for d in range(2):
        raw = dot(src4, wd_ref[:, 128 + 128 * d : 256 + 128 * d])
        step[d * HT : d * HT + HT, :] = softplus(raw + biasc[d : d + 1, :])

    for d in range(2):
        for q in range(8):
            at = slice(q * 512, q * 512 + 512)
            bc[d * HT : d * HT + HT, at] = dot(src4, sel[1 + d, :, at])

    every("row", r4, c_s, c_r).wait_recv()
    for s in range(R):
        cells = r4[s].astype(F32)
        for w in range(8):
            x2[pl.ds(64 * s + w, 8, stride=8), :] = cells[8 * w : 8 * w + 8, :]

    for d in range(2):
        rate_d = ratec[d] * -LOG2E
        rates_d = [rate_d[n : n + 1, :] for n in range(N)]

        def col_body(i, states):
            block = i if d == 0 else R // 2 - 1 - i
            order = range(16) if d == 0 else range(15, -1, -1)
            rows = [pl.multiple_of(d * HT + block * 128 + 8 * u, 8) for u in order]
            x_rows = [pl.multiple_of(block * 128 + 8 * u, 8) for u in order]
            return scan_block(states, rows, x_rows, step, x2, bc, rates_d, put)

        lax.fori_loop(0, R // 2, col_body, zero_states)

    for b in range(R):
        out_ref[64 * b : 64 * b + 64, :] = (
            y2[64 * b : 64 * b + 64, :] + y2[HT + 64 * b : HT + 64 * b + 64, :]).astype(BF16)

    every("row", s4, q_s, q_r).wait_send()
    every("row", s4, c_s, c_r).wait_send()


def local(R, C, features, gate_branch, w_row_proj, w_dt_row, dt_bias_row, rate_row, skip_row,
          conv_kernel, conv_bias, w_col_proj, w_dt_col, dt_bias_col, rate_col):
    E = features.shape[2]
    dma = pltpu.SemaphoreType.DMA
    TW = 4 * C
    out = pl.pallas_call(
        functools.partial(kernel, R, C),
        out_shape=jax.ShapeDtypeStruct((64 * R, 128), BF16),
        in_specs=[pl.BlockSpec(memory_space=pltpu.HBM)] * 13,
        out_specs=pl.BlockSpec(memory_space=pltpu.VMEM),
        scratch_shapes=[
            pltpu.VMEM((64, E), BF16),
            pltpu.VMEM((64, E), BF16),
            pltpu.VMEM((E, 128), BF16),
            pltpu.VMEM((2, 32, 64), BF16),
            pltpu.VMEM((2, 64), F32),
            pltpu.VMEM((2, N, 64), F32),
            pltpu.VMEM((1, 64), F32),
            pltpu.VMEM((3, 3, 64), F32),
            pltpu.VMEM((1, 64), F32),
            pltpu.VMEM((E, 128), BF16),
            pltpu.VMEM((2, 32, 128), BF16),
            pltpu.VMEM((2, 128), F32),
            pltpu.VMEM((2, N, 128), F32),
            pltpu.VMEM((128, 384), BF16),
            dma((13,)),
            pltpu.VMEM((C, 32, 128), BF16),
            pltpu.VMEM((C, 32, 128), BF16),
            pltpu.VMEM((C, 32, 128), BF16),
            pltpu.VMEM((C, 32, 128), BF16),
            pltpu.VMEM((2, C // 2, 64, 128), BF16),
            pltpu.VMEM((64 * C, 128), BF16),
            pltpu.VMEM((2, TW, 128), BF16),
            pltpu.VMEM((2, TW, 128), BF16),
            pltpu.VMEM((C, 32, 128), BF16),
            pltpu.VMEM((C, 32, 128), BF16),
            pltpu.VMEM((R, 64, 128), BF16),
            pltpu.VMEM((R, 64, 128), BF16),
            pltpu.VMEM((R, 64, 128), BF16),
            pltpu.VMEM((3, 128, 4096), BF16),
            pltpu.VMEM((64 * C, 4096), F32),
            pltpu.VMEM((64 * C, 128), F32),
            pltpu.VMEM((64 * C, 128), F32),
            pltpu.VMEM((64 * C, 128), F32),
            pltpu.VMEM((64, 128), F32),
            pltpu.VMEM((32 * C + 16, 128), F32),
            pltpu.VMEM((32 * C, 128), F32),
            pltpu.VMEM((TW + 16, 128), F32),
            dma, dma, dma, dma, dma, dma, dma, dma, dma((2,)), dma((2,)), dma, dma, dma, dma, dma, dma,
        ],
        compiler_params=pltpu.CompilerParams(
            collective_id=0, has_side_effects=True, vmem_limit_bytes=40 << 20),
    )(*(pltpu.with_memory_space_constraint(v, pltpu.HBM) for v in (
        features.reshape(64, E), gate_branch.reshape(64, E), w_row_proj, w_dt_row, dt_bias_row,
        jnp.transpose(rate_row, (0, 2, 1)), skip_row.reshape(1, 64), conv_kernel,
        conv_bias.reshape(1, 64), w_col_proj, w_dt_col, dt_bias_col,
        jnp.transpose(rate_col, (0, 2, 1)))))
    return out.reshape(8 * R, 8, 128)


def solution(mesh):
    return jax.shard_map(
        functools.partial(local, mesh.shape["row"], mesh.shape["col"]),
        mesh=mesh,
        in_specs=(
            P("row", "col", None),
            P("row", "col", None),
            P(),
            P(None, None, "col"),
            P(None, "col"),
            P(None, "col", None),
            P("col"),
            P(None, None, "col"),
            P("col"),
            P(),
            P(None, None, "row"),
            P(None, "row"),
            P(None, "row", None),
        ),
        out_specs=P(None, "col", "row"),
        check_vma=False,
    )
```

```python
import functools

import jax
import jax.numpy as jnp
from jax import lax
from jax.experimental import pallas as pl
from jax.experimental.pallas import tpu as pltpu
from jax.sharding import PartitionSpec as P

F32, BF16 = jnp.float32, jnp.bfloat16
MESH = pl.DeviceIdType.MESH
N = 16
LOG2E = 1.4426950408889634


def softplus(v):
    return jnp.maximum(v, 0.0) + jnp.log1p(jnp.exp(-jnp.abs(v)))


def silu(v):
    return v / (1.0 + jnp.exp(-v))


def turn(v):
    groups = v.shape[0] // 8
    return jnp.concatenate([v[8 * g : 8 * g + 8] for g in reversed(range(groups))], axis=0)


def swap(v):
    return pltpu.roll(v, 64, 1)


def dot(a, b):
    return jnp.dot(a, b, preferred_element_type=F32)


def scan_block(states, rows, x_rows, step_ref, x_ref, bc_ref, rates, emit):
    states = list(states)
    for row, x_row in zip(rows, x_rows):
        step = step_ref[pl.ds(row, 8), :]
        drive = step * x_ref[pl.ds(x_row, 8), :]
        out = None
        for n in range(N):
            decay = jnp.exp2(step * rates[n])
            states[n] = decay * states[n] + drive * bc_ref[pl.ds(row, 8), n * 128 : (n + 1) * 128]
            term = states[n] * bc_ref[pl.ds(row, 8), (N + n) * 128 : (N + n + 1) * 128]
            out = term if out is None else out + term
        emit(row, out)
    return tuple(states)


def kernel(
    R, C,
    f_hbm, g_hbm, wrp_hbm, wdtr_hbm, biasr_hbm, rater_hbm, skip_hbm, kern_hbm, biask_hbm, wcp_hbm,
    wdtc_hbm, biasc_hbm, ratec_hbm,
    out_ref,
    f_ref, g_ref, wrp_ref, wdtr, biasr, rater, skipr, kern, biask, wcp_ref, wdtc, biasc, ratec,
    wd_ref, load_sem,
    sx, rx, sgx, rg, rp, srcs, sh, rh, s3, r3, s4, r4, rp4,
    sel, bc, step, x2, y2, lay, z, acc, hz,
    px_s, px_r, pg_s, pg_r, pp_s, pp_r, pf_s, pf_r, h_s, h_r, m_s, m_r, c_s, c_r, q_s, q_r,
):
    r, c = lax.axis_index("row"), lax.axis_index("col")
    half = C // 2
    chip, core = lax.div(c, 2), lax.rem(c, 2)
    TW = half * 8
    lane = lax.broadcasted_iota(jnp.int32, (1, 128), 1)
    low = lane < 64

    def col_copy(src, dst, ss, rs, slot_src, slot_dst, to):
        return pltpu.make_async_remote_copy(
            src_ref=src.at[slot_src], dst_ref=dst.at[slot_dst], send_sem=ss, recv_sem=rs,
            device_id={"col": to}, device_id_type=MESH)

    def row_copy(src, dst, ss, rs, slot_src, slot_dst, to):
        return pltpu.make_async_remote_copy(
            src_ref=src.at[slot_src], dst_ref=dst.at[slot_dst], send_sem=ss, recv_sem=rs,
            device_id={"row": to}, device_id_type=MESH)

    def send(axis, src, dst, ss, rs, own):
        me, size = (c, C) if axis == "col" else (r, R)
        for k in range(1, size):
            to = lax.rem(me + k, size)
            pltpu.make_async_remote_copy(
                src_ref=src.at[me if own else to], dst_ref=dst.at[me], send_sem=ss, recv_sem=rs,
                device_id={axis: to}, device_id_type=MESH).start()

    def every(axis, ref, ss, rs):
        me, size = (c, C) if axis == "col" else (r, R)
        some = ref.at[pl.ds(0, size - 1)]
        return pltpu.make_async_remote_copy(
            src_ref=some, dst_ref=some, send_sem=ss, recv_sem=rs,
            device_id={axis: lax.rem(me + 1, size)}, device_id_type=MESH)

    sources = (f_hbm, wrp_hbm, g_hbm, wdtr_hbm, biasr_hbm, rater_hbm, skip_hbm, kern_hbm, biask_hbm,
               wcp_hbm, wdtc_hbm, biasc_hbm, ratec_hbm)
    targets = (f_ref, wrp_ref, g_ref, wdtr, biasr, rater, skipr, kern, biask,
               wcp_ref, wdtc, biasc, ratec)
    loads = [pltpu.make_async_copy(a, b, load_sem.at[i])
             for i, (a, b) in enumerate(zip(sources, targets))]
    for load in loads[:3]:
        load.start()

    barrier = pltpu.get_barrier_semaphore()
    for k in range(1, C):
        pl.semaphore_signal(barrier, inc=1, device_id={"col": lax.rem(c + k, C)}, device_id_type=MESH)
    for k in range(1, R):
        pl.semaphore_signal(barrier, inc=1, device_id={"row": lax.rem(r + k, R)}, device_id_type=MESH)

    for load in loads[3:]:
        load.start()

    ta = lax.broadcasted_iota(jnp.int32, (64, 64), 0)
    tb = lax.broadcasted_iota(jnp.int32, (64, 64), 1)
    perm = jnp.where(tb == lax.rem(ta, 8) * 8 + lax.div(ta, 8), 1.0, 0.0).astype(BF16)

    def packed(v):
        near, far = v[0:32, :], turn(v[32:64, :])
        return jnp.where(low, near, swap(far)).astype(BF16), jnp.where(low, swap(near), far).astype(BF16)

    loads[0].wait()
    loads[1].wait()
    proj = dot(f_ref[...], wrp_ref[...]).astype(BF16).astype(F32)
    for h in range(8):
        lay[pl.ds(h, 8, stride=8), :] = proj[8 * h : 8 * h + 8, :]
    rp[core, chip] = lay[...].astype(BF16)
    turned = dot(perm, f_ref[...])
    for j in range(half):
        sx[2 * j], sx[2 * j + 1] = packed(turned[:, 128 * j : 128 * j + 128])

    pl.semaphore_wait(barrier, C - 1 + R - 1)
    for k in range(1, half):
        pltpu.make_async_remote_copy(
            src_ref=rp.at[core, chip], dst_ref=rp.at[core, chip], send_sem=pp_s, recv_sem=pp_r,
            device_id={"col": lax.rem(c + 2 * k, C)}, device_id_type=MESH).start()
    send("col", sx, rx, px_s, px_r, False)
    loads[2].wait()
    turned = dot(perm, g_ref[...])
    for j in range(half):
        sgx[2 * j], sgx[2 * j + 1] = packed(turned[:, 128 * j : 128 * j + 128])
    rx[c] = sx[c]
    rg[c] = sgx[c]

    kk = lax.broadcasted_iota(jnp.int32, (128, 128), 0)
    ll = lax.broadcasted_iota(jnp.int32, (128, 128), 1)
    kl = kk - jnp.where(ll >= 64, 64, 0)
    for n in range(2 * N):
        at = slice(n * 128, n * 128 + 128)
        sel[0, :, at] = jnp.where(kl == 32 + n, 1.0, 0.0).astype(BF16)
        sel[1, :, at] = jnp.where(kk == 32 + n, 1.0, 0.0).astype(BF16)
        sel[2, :, at] = jnp.where(kk == 96 + n, 1.0, 0.0).astype(BF16)

    for load in loads[3:]:
        load.wait()
    ea = lax.broadcasted_iota(jnp.int32, (64, 128), 0)
    eb = lax.broadcasted_iota(jnp.int32, (64, 128), 1)
    wd_ref[...] = jnp.zeros((128, 384), BF16)
    wd_ref[0:32, 0:128] = dot(wdtr[0], jnp.where(ea == eb, 1.0, 0.0).astype(BF16)).astype(BF16)
    wd_ref[64:96, 0:128] = dot(wdtr[1], jnp.where(ea == eb - 64, 1.0, 0.0).astype(BF16)).astype(BF16)
    wd_ref[0:32, 128:256] = wdtc[0]
    wd_ref[64:96, 256:384] = wdtc[1]

    def beside(a, b):
        return jnp.concatenate([a, b], axis=1)

    bias_row = beside(biasr[0:1, :], biasr[1:2, :])
    skip = beside(skipr[...], skipr[...])
    conv_bias = beside(biask[...], biask[...])
    taps = [[beside(kern[i, j : j + 1, :], kern[i, 2 - j : 3 - j, :]) for j in range(3)] for i in range(3)]
    rate_all = beside(rater[0], rater[1]) * -LOG2E

    direct = rp.at[core, pl.ds(0, half - 1)]
    peers = pltpu.make_async_remote_copy(
        src_ref=direct, dst_ref=direct, send_sem=pp_s, recv_sem=pp_r,
        device_id={"col": c + 1 - 2 * core}, device_id_type=MESH)
    peers.wait_recv()
    passed = pltpu.make_async_remote_copy(
        src_ref=rp.at[core], dst_ref=rp.at[core], send_sem=pf_s, recv_sem=pf_r,
        device_id={"col": c + 1 - 2 * core}, device_id_type=MESH)
    passed.start()
    send("col", sgx, rg, pg_s, pg_r, False)
    passed.wait_recv()
    for b in range(half):
        o = C - 1 - b
        pb, po = rp[b % 2, b // 2].astype(F32), rp[o % 2, o // 2].astype(F32)
        srcs[64 * b : 64 * b + 64, :] = jnp.where(low, pb, turn(po)).astype(BF16)
        srcs[64 * o : 64 * o + 64, :] = jnp.where(low, po, turn(pb)).astype(BF16)
    step[...] = softplus(dot(srcs[...], wd_ref[:, 0:128]) + bias_row)

    for q in range(8):
        at = slice(q * 512, q * 512 + 512)
        bc[:, at] = dot(srcs[...], sel[0, :, at])

    def facing(ref, b):
        one, two = ref[b].astype(F32), ref[C - 1 - b].astype(F32)
        p, q = jnp.where(low, one, two), jnp.where(low, two, one)
        return p, turn(swap(q)), q, turn(swap(p))

    every("col", rx, px_s, px_r).wait_recv()
    for b in range(half):
        o = C - 1 - b
        parts = facing(rx, b)
        x2[64 * b : 64 * b + 32, :], x2[64 * b + 32 : 64 * b + 64, :] = parts[0], parts[1]
        x2[64 * o : 64 * o + 32, :], x2[64 * o + 32 : 64 * o + 64, :] = parts[2], parts[3]

    rates = [rate_all[n : n + 1, :] for n in range(N)]
    zero_states = tuple(jnp.zeros((8, 128), F32) for _ in range(N))

    def put(row, out):
        y2[pl.ds(row, 8), :] = out

    def row_body(i, states):
        rows = [pl.multiple_of(i * 128 + 8 * u, 8) for u in range(16)]
        return scan_block(states, rows, rows, step, x2, bc, rates, put)

    lax.fori_loop(0, C // 2, row_body, zero_states)

    every("col", rg, pg_s, pg_r).wait_recv()
    z[0:8, :] = jnp.zeros((8, 128), F32)
    for b in range(half):
        here, there = slice(64 * b, 64 * b + 64), slice(64 * (C - 1 - b), 64 * (C - b))
        mix = skip * x2[here, :] + y2[here, :] + swap(turn(y2[there, :]))
        gate = jnp.concatenate(facing(rg, b)[:2], axis=0)
        gated = (mix * silu(gate)).astype(BF16).astype(F32)
        z[64 * b + 8 : 64 * b + 72, :] = gated
    z[8 * TW + 8 : 8 * TW + 16, :] = swap(z[8 * TW : 8 * TW + 8, :])

    sh[0] = z[pl.ds(8 + 7, TW, stride=8), :].astype(BF16)
    sh[1] = z[pl.ds(8, TW, stride=8), :].astype(BF16)
    down = row_copy(sh, rh, h_s.at[0], h_r.at[0], 0, 0, lax.rem(r + 1, R))
    up = row_copy(sh, rh, h_s.at[1], h_r.at[1], 1, 1, lax.rem(r + R - 1, R))

    @pl.when(r < R - 1)
    def _():
        down.start()

    @pl.when(r > 0)
    def _():
        up.start()

    sub = lax.broadcasted_iota(jnp.int32, (8, 128), 0)

    @pl.loop(0, half)
    def _(b):
        group = [z[pl.ds(pl.multiple_of(b * 64 + 8 * u, 8), 8), :] for u in range(10)]
        for u in range(8):
            q = [taps[i][0] * group[u] + taps[i][1] * group[u + 1] + taps[i][2] * group[u + 2]
                 for i in range(3)]
            above = jnp.where(sub == 0, 0.0, pltpu.roll(q[0], 1, 0))
            below = jnp.where(sub == 7, 0.0, pltpu.roll(q[2], 7, 0))
            acc[pl.ds(pl.multiple_of(b * 64 + 8 * u, 8), 8), :] = conv_bias + above + q[1] + below

    peers.wait_send()
    passed.wait_send()
    every("col", sx, px_s, px_r).wait_send()
    every("col", sgx, pg_s, pg_r).wait_send()
    @pl.when(r == 0)
    def _():
        rh[0] = jnp.zeros((TW, 128), BF16)

    @pl.when(r == R - 1)
    def _():
        rh[1] = jnp.zeros((TW, 128), BF16)

    @pl.when(r > 0)
    def _():
        down.wait_recv()

    @pl.when(r < R - 1)
    def _():
        up.wait_recv()

    for side, i, first in ((0, 0, 0), (1, 2, 7)):
        hz[0:8, :] = jnp.zeros((8, 128), F32)
        halo = rh[side].astype(F32)
        hz[8 : 8 + TW, :] = halo
        hz[8 + TW : 16 + TW, :] = swap(jnp.broadcast_to(halo[TW - 1 : TW, :], (8, 128)))
        add = (taps[i][0] * hz[7 : 7 + TW, :] + taps[i][1] * halo + taps[i][2] * hz[9 : 9 + TW, :])
        at = pl.ds(first, TW, stride=8)
        acc[at, :] = acc[at, :] + add

    for b in range(half):
        cells = silu(acc[64 * b : 64 * b + 64, :]).astype(BF16).astype(F32)
        near, far = cells[0:32, :], swap(turn(cells[32:64, :]))
        s3[b] = jnp.where(low, near, far).astype(BF16)
        s3[C - 1 - b] = jnp.where(low, far, near).astype(BF16)

    send("col", s3, r3, m_s, m_r, False)
    r3[c] = s3[c]
    every("col", r3, m_s, m_r).wait_recv()

    tokens = []
    for j in range(R):
        one, two = r3[2 * j].astype(F32), r3[2 * j + 1].astype(F32)
        tokens.append(jnp.concatenate(
            [jnp.where(low, one, swap(two)), turn(jnp.where(low, swap(one), two))], axis=0).astype(BF16))
        s4[j] = tokens[j]
    proj = dot(jnp.concatenate(tokens, axis=1), wcp_ref[...]).astype(BF16).astype(F32)
    for w in range(8):
        lay[pl.ds(w, 8, stride=8), :] = proj[8 * w : 8 * w + 8, :]
    rp4[r] = lay[...].astype(BF16)
    send("row", rp4, rp4, q_s, q_r, True)
    send("row", s4, r4, c_s, c_r, False)
    r4[r] = s4[r]
    every("col", s3, m_s, m_r).wait_send()

    @pl.when(r < R - 1)
    def _():
        down.wait_send()

    @pl.when(r > 0)
    def _():
        up.wait_send()

    HT = 64 * R

    every("row", rp4, q_s, q_r).wait_recv()
    src4 = rp4[...].reshape(HT, 128)
    for d in range(2):
        raw = dot(src4, wd_ref[:, 128 + 128 * d : 256 + 128 * d])
        step[d * HT : d * HT + HT, :] = softplus(raw + biasc[d : d + 1, :])

    for d in range(2):
        for q in range(8):
            at = slice(q * 512, q * 512 + 512)
            bc[d * HT : d * HT + HT, at] = dot(src4, sel[1 + d, :, at])

    every("row", r4, c_s, c_r).wait_recv()
    for s in range(R):
        cells = r4[s].astype(F32)
        for w in range(8):
            x2[pl.ds(64 * s + w, 8, stride=8), :] = cells[8 * w : 8 * w + 8, :]

    for d in range(2):
        rate_d = ratec[d] * -LOG2E
        rates_d = [rate_d[n : n + 1, :] for n in range(N)]

        def col_body(i, states):
            block = i if d == 0 else R // 2 - 1 - i
            order = range(16) if d == 0 else range(15, -1, -1)
            rows = [pl.multiple_of(d * HT + block * 128 + 8 * u, 8) for u in order]
            x_rows = [pl.multiple_of(block * 128 + 8 * u, 8) for u in order]
            return scan_block(states, rows, x_rows, step, x2, bc, rates_d, put)

        lax.fori_loop(0, R // 2, col_body, zero_states)

    for b in range(R):
        out_ref[64 * b : 64 * b + 64, :] = (
            y2[64 * b : 64 * b + 64, :] + y2[HT + 64 * b : HT + 64 * b + 64, :]).astype(BF16)

    every("row", s4, q_s, q_r).wait_send()
    every("row", s4, c_s, c_r).wait_send()


def local(R, C, features, gate_branch, w_row_proj, w_dt_row, dt_bias_row, rate_row, skip_row,
          conv_kernel, conv_bias, w_col_proj, w_dt_col, dt_bias_col, rate_col):
    E = features.shape[2]
    dma = pltpu.SemaphoreType.DMA
    TW = 4 * C
    out = pl.pallas_call(
        functools.partial(kernel, R, C),
        out_shape=jax.ShapeDtypeStruct((64 * R, 128), BF16),
        in_specs=[pl.BlockSpec(memory_space=pltpu.HBM)] * 13,
        out_specs=pl.BlockSpec(memory_space=pltpu.VMEM),
        scratch_shapes=[
            pltpu.VMEM((64, E), BF16),
            pltpu.VMEM((64, E), BF16),
            pltpu.VMEM((E, 128), BF16),
            pltpu.VMEM((2, 32, 64), BF16),
            pltpu.VMEM((2, 64), F32),
            pltpu.VMEM((2, N, 64), F32),
            pltpu.VMEM((1, 64), F32),
            pltpu.VMEM((3, 3, 64), F32),
            pltpu.VMEM((1, 64), F32),
            pltpu.VMEM((E, 128), BF16),
            pltpu.VMEM((2, 32, 128), BF16),
            pltpu.VMEM((2, 128), F32),
            pltpu.VMEM((2, N, 128), F32),
            pltpu.VMEM((128, 384), BF16),
            dma((13,)),
            pltpu.VMEM((C, 32, 128), BF16),
            pltpu.VMEM((C, 32, 128), BF16),
            pltpu.VMEM((C, 32, 128), BF16),
            pltpu.VMEM((C, 32, 128), BF16),
            pltpu.VMEM((2, C // 2, 64, 128), BF16),
            pltpu.VMEM((64 * C, 128), BF16),
            pltpu.VMEM((2, TW, 128), BF16),
            pltpu.VMEM((2, TW, 128), BF16),
            pltpu.VMEM((C, 32, 128), BF16),
            pltpu.VMEM((C, 32, 128), BF16),
            pltpu.VMEM((R, 64, 128), BF16),
            pltpu.VMEM((R, 64, 128), BF16),
            pltpu.VMEM((R, 64, 128), BF16),
            pltpu.VMEM((3, 128, 4096), BF16),
            pltpu.VMEM((64 * C, 4096), F32),
            pltpu.VMEM((64 * C, 128), F32),
            pltpu.VMEM((64 * C, 128), F32),
            pltpu.VMEM((64 * C, 128), F32),
            pltpu.VMEM((64, 128), F32),
            pltpu.VMEM((32 * C + 16, 128), F32),
            pltpu.VMEM((32 * C, 128), F32),
            pltpu.VMEM((TW + 16, 128), F32),
            dma, dma, dma, dma, dma, dma, dma, dma, dma((2,)), dma((2,)), dma, dma, dma, dma, dma, dma,
        ],
        compiler_params=pltpu.CompilerParams(
            collective_id=0, has_side_effects=True, vmem_limit_bytes=40 << 20),
    )(*(pltpu.with_memory_space_constraint(v, pltpu.HBM) for v in (
        features.reshape(64, E), gate_branch.reshape(64, E), w_row_proj, w_dt_row, dt_bias_row,
        jnp.transpose(rate_row, (0, 2, 1)), skip_row.reshape(1, 64), conv_kernel,
        conv_bias.reshape(1, 64), w_col_proj, w_dt_col, dt_bias_col,
        jnp.transpose(rate_col, (0, 2, 1)))))
    return out.reshape(8 * R, 8, 128)


def solution(mesh):
    return jax.shard_map(
        functools.partial(local, mesh.shape["row"], mesh.shape["col"]),
        mesh=mesh,
        in_specs=(
            P("row", "col", None),
            P("row", "col", None),
            P(),
            P(None, None, "col"),
            P(None, "col"),
            P(None, "col", None),
            P("col"),
            P(None, None, "col"),
            P("col"),
            P(),
            P(None, None, "row"),
            P(None, "row"),
            P(None, "row", None),
        ),
        out_specs=P(None, "col", "row"),
        check_vma=False,
    )
```
